1024 devices in a mesh: rep: 128 (over z, y), tp: 8 (over x, core).
Axes of the slice: x: 4, y: 4, z: 32, core: 2. Of those that a mesh axis runs over, the one named last changes fastest.
Arguments:
- tokens: bfloat16 [131072, 4096], P('rep', 'tp'), may hold values from -6 to 6
- key_grad: bfloat16 [131072, 512], P('rep', 'tp'), may hold values from -0.19921875 to 0.19921875
- momentum: float32 [128, 4096, 512], P('rep', 'tp'), may hold values from -6 to 6
- key_weight: bfloat16 [4096, 512], P('tp'), may hold values from -4 to 4
- target: bfloat16 [4096, 512], P('tp'), may hold values from -4 to 4
- positions: int32 [64, 8, 64], P('tp'), may hold values from 0 to 4095, as said below
Outputs:
- update: float32 [4096, 512], P('tp')
- residual: float32 [128, 4096, 512], P('rep', 'tp')
- blended: bfloat16 [4096, 512], P('tp')
The draws below stay inside these ranges and needn't reach their ends.
Inputs may be any that keep to these rules, and one draw needn't show every extreme that they name: The 64 positions of each block are distinct coefficient numbers of that block.
All inputs are finite; a program needn't handle non-finite values.
Results may differ from the reference program's by a relative error of at most 0.0054.
Values may be sent and summed in bfloat16 or wider, within the bound.
A program may use at most 64 MiB of HBM per device.

```python
import jax
import jax.numpy as jnp
from jax import lax

DW = 4096
KV = 512
BLOCK = 64
KEEP = 64
TOK_DEV = 1024
TOKENS = 131072
N_REP = 128


def draw_positions(key, part):
    key = jax.random.fold_in(key, 11)
    count = DW // BLOCK * (KV // BLOCK)
    keys = jax.random.split(key, count)

    def pick(single):
        return jax.random.permutation(single, BLOCK * BLOCK)[:KEEP]
    chosen = jax.vmap(pick)(keys)
    return chosen.reshape(DW // BLOCK, KV // BLOCK, KEEP).astype(jnp.int32)


def block_scale(rng, dims, pieces, smallest, high):
    level, own = 1.0, jax.random.fold_in(rng, 6)
    for axis_at, blocks in pieces:
        draws = jnp.exp(jax.random.uniform(jax.random.fold_in(own, axis_at), (blocks,), jnp.float32, smallest / len(pieces), high / len(pieces)))
        level = level * jnp.repeat(draws, dims[axis_at] // blocks).reshape([-1 if axis == axis_at else 1 for axis in range(len(dims))])
    return level


def normal_values(stream_key, dims, width, most, pieces=(), held_as=jnp.bfloat16):
    result = jax.random.normal(stream_key, dims, jnp.float32) * width
    if len(pieces) > 0:
        result = block_scale(stream_key, dims, pieces, -0.22, 0.18) * result
    return jnp.clip(result, min=-most, max=most).astype(held_as)


def setup_inputs(seed: int = 0) -> dict:
    splits = jax.random.split(jax.random.key(seed), 7)
    tokens = normal_values(splits[0], (TOKENS, DW), 1.0, 6.0, ((0, 128), (1, 8)))
    key_grad = normal_values(splits[1], (TOKENS, KV), 0.03, 0.19921875, ((0, 128), (1, 8)))
    momentum = normal_values(splits[2], (N_REP, DW, KV), 1.0, 6.0, ((0, 128), (1, 8)), jnp.float32)
    key_weight = normal_values(splits[3], (DW, KV), 1.0, 4.0, ((0, 8),))
    target = normal_values(splits[4], (DW, KV), 1.0, 4.0, ((0, 8),))
    positions = draw_positions(jax.random.fold_in(splits[6], 71), 0)
    return {"tokens": tokens, "key_grad": key_grad, "momentum": momentum, "key_weight": key_weight, "target": target, "positions": positions}


momentum_decay = 0.9
polyak_rate = 0.25
update_rate = 0.1

def cosine_table(length):
    index = jnp.arange(length).astype(jnp.float32)
    angle_grid = jnp.pi * (2.0 * index[None, :] + 1.0) * index[:, None] / (2.0 * length)
    scales = jnp.where(index == 0, jnp.sqrt(1.0 / length), jnp.sqrt(2.0 / length))
    return scales[:, None] * jnp.cos(angle_grid)

def to_spectrum(field, table):
    height, breadth = field.shape
    blocked = field.reshape(height // BLOCK, BLOCK, breadth // BLOCK, BLOCK)
    spectrum = jnp.einsum('ai,pibj,cj->pbac', table, blocked, table, precision=lax.Precision.HIGHEST)
    return spectrum.reshape(height // BLOCK, breadth // BLOCK, BLOCK * BLOCK)

def from_spectrum(spectrum, table):
    row_blocks, col_blocks, _ = spectrum.shape
    square = spectrum.reshape(row_blocks, col_blocks, BLOCK, BLOCK)
    field = jnp.einsum('ai,pbac,cj->pibj', table, square, table, precision=lax.Precision.HIGHEST)
    return field.reshape(row_blocks * BLOCK, col_blocks * BLOCK)

def scatter_kept(values, positions):
    row_blocks, col_blocks, _ = values.shape
    first = jnp.arange(row_blocks).astype(jnp.int32)[:, None, None]
    second = jnp.arange(col_blocks).astype(jnp.int32)[None, :, None]
    empty = jnp.zeros((row_blocks, col_blocks, BLOCK * BLOCK), jnp.float32)
    return empty.at[first, second, positions.astype(jnp.int32)].set(values)

def reference(tokens, key_grad, momentum, key_weight, target, positions):
    table = cosine_table(BLOCK)

    def replica(inputs):
        token_rows, grad_rows, state = inputs
        gradient = jnp.dot(token_rows.T, grad_rows, preferred_element_type=jnp.float32)
        moment = momentum_decay * state + gradient
        kept = jnp.take_along_axis(to_spectrum(moment, table), positions, axis=2)
        residual = moment - from_spectrum(scatter_kept(kept, positions), table)
        return (kept, residual)
    kept_all, residual = lax.map(replica, (tokens.reshape(N_REP, TOK_DEV, DW), key_grad.reshape(N_REP, TOK_DEV, KV), momentum))
    total = lax.optimization_barrier(jnp.sum(kept_all, axis=0))
    update = from_spectrum(scatter_kept(total, positions), table)
    blended = (1.0 - polyak_rate) * target.astype(jnp.float32) + polyak_rate * (key_weight.astype(jnp.float32) - update_rate * update)
    return (update, residual, blended.astype(jnp.bfloat16))
```

```python
import functools

import jax
import jax.numpy as jnp
import ml_dtypes
import numpy as np
from jax import lax
from jax.experimental import pallas as pl
from jax.experimental.pallas import tpu as pltpu
from jax.sharding import PartitionSpec as P

BLOCK = 64
LANES = 128
NX, NY = 4, 4

momentum_decay = 0.9
polyak_rate = 0.25
update_rate = 0.1

MESH = pl.DeviceIdType.MESH
NT = (((1,), (1,)), ((), ()))


def split_table():
    index = np.arange(BLOCK, dtype=np.float64)
    angle = np.pi * (2.0 * index[:, None] + 1.0) * index[None, :] / (2.0 * BLOCK)
    scale = np.where(index == 0, np.sqrt(1.0 / BLOCK), np.sqrt(2.0 / BLOCK))
    table = np.cos(angle) * scale[None, :]
    high = table.astype(ml_dtypes.bfloat16)
    low = (table - high.astype(np.float64)).astype(ml_dtypes.bfloat16)
    return np.concatenate([high, low], axis=0)


def split_rows(value):
    high = value.astype(jnp.bfloat16)
    low = (value - high.astype(jnp.float32)).astype(jnp.bfloat16)
    return high, low


def strip_of(strip):
    return pl.ds(pl.multiple_of(strip * LANES, LANES), LANES)


def make_bases(pos_ref, table_ref, at_ref, w_ref):
    row_blocks, col_blocks, keep = pos_ref.shape
    width = col_blocks * keep
    lane = lax.broadcasted_iota(jnp.int32, (BLOCK, LANES), 1)
    level = lax.broadcasted_iota(jnp.int32, (BLOCK, width), 0)
    table = table_ref[...]
    flat = jnp.concatenate([pos_ref[:, b, :] for b in range(col_blocks)], axis=1)
    for p in range(row_blocks):
        row = flat[p : p + 1, :]
        first = jnp.where(level == (row >> 6), 1.0, 0.0).astype(jnp.bfloat16)
        second = jnp.where(level == (row & 63), 1.0, 0.0).astype(jnp.bfloat16)
        picked = jnp.dot(table, first, preferred_element_type=jnp.float32)
        at_ref[p] = picked[:BLOCK] + picked[BLOCK:]
        other = jnp.dot(table, second, preferred_element_type=jnp.float32)
        for g in range(width // LANES):
            for part in range(2):
                piece = other[part * BLOCK : (part + 1) * BLOCK, g * LANES : (g + 1) * LANES]
                top = jnp.where(lane < BLOCK, piece, 0.0).astype(jnp.bfloat16)
                low = jnp.where(lane < BLOCK, 0.0, piece).astype(jnp.bfloat16)
                w_ref[p, g, 0:BLOCK, part * LANES : (part + 1) * LANES] = top
                w_ref[p, g, BLOCK : 2 * BLOCK, part * LANES : (part + 1) * LANES] = low


def encode(block, at, w):
    high, low = split_rows(block)
    both = jnp.dot(jnp.concatenate([high, low], axis=0), w, preferred_element_type=jnp.float32)
    mixed = both[:BLOCK, :LANES] + both[:BLOCK, LANES:] + both[BLOCK:, :LANES]
    return jnp.sum(mixed * at, axis=0, keepdims=True)


def decode(values, at, w):
    high, low = split_rows(at * values)
    rows = jnp.concatenate(
        [jnp.concatenate([high, high], axis=1), jnp.concatenate([low, jnp.zeros_like(low)], axis=1)], axis=0
    )
    both = lax.dot_general(rows, w, NT, preferred_element_type=jnp.float32)
    return both[:BLOCK] + both[BLOCK:]


def first_kernel(
    ny, nz,
    tok_hbm, grad_hbm, mom_hbm, pos_hbm, table_hbm,
    res_hbm, total_hbm, at_hbm, w_hbm,
    tok, tok_t, gall, mom, at, w, pos, table, kept, part, ybuf, total,
    load_sem, send_sem, recv_sem, z_send, z_recv, y_send, y_recv, out_sem,
):
    rep, tp = lax.axis_index("rep"), lax.axis_index("tp")
    z, y = rep // ny, lax.rem(rep, ny)
    x, core = tp // 2, lax.rem(tp, 2)
    right = lax.rem(x + 1, NX) * 2 + core
    left = lax.rem(x + NX - 1, NX) * 2 + core
    far = lax.rem(x + 2, NX) * 2 + core
    other = 2 * x + 1 - core
    rows_p = at.shape[0]
    chunk = kept.shape[0] // nz

    loads = [
        pltpu.make_async_copy(pos_hbm, pos, load_sem.at[0]),
        pltpu.make_async_copy(table_hbm, table, load_sem.at[1]),
        pltpu.make_async_copy(grad_hbm, gall.at[pl.ds(pl.multiple_of(tp * BLOCK, BLOCK), BLOCK)], load_sem.at[2]),
        pltpu.make_async_copy(tok_hbm, tok, load_sem.at[3]),
        pltpu.make_async_copy(mom_hbm, mom, load_sem.at[4]),
    ]
    for load in loads:
        load.start()

    barrier = pltpu.get_barrier_semaphore()
    for peer in (right, left, other):
        pl.semaphore_signal(barrier, inc=1, device_id={"tp": peer}, device_id_type=MESH)

    def greet_z(step, carry):
        peer = lax.rem(z + step, nz) * ny + y
        pl.semaphore_signal(barrier, inc=1, device_id={"rep": peer}, device_id_type=MESH)
        return carry

    def greet_y(step, carry):
        peer = z * ny + lax.rem(y + step, ny)
        pl.semaphore_signal(barrier, inc=1, device_id={"rep": peer}, device_id_type=MESH)
        return carry

    lax.fori_loop(1, nz, greet_z, 0)
    lax.fori_loop(1, ny, greet_y, 0)

    loads[0].wait()
    loads[1].wait()
    make_bases(pos, table, at, w)
    bases_out = [
        pltpu.make_async_copy(at, at_hbm, out_sem.at[0]),
        pltpu.make_async_copy(w, w_hbm, out_sem.at[1]),
    ]
    for copy in bases_out:
        copy.start()

    pl.semaphore_wait(barrier, 3 + (nz - 1) + (ny - 1))

    half = BLOCK // 2

    def rows(owner, part_at):
        return gall.at[pl.ds(pl.multiple_of(owner * BLOCK + part_at * half, half), half)]

    def send(number, source, target, device):
        copy = pltpu.make_async_remote_copy(
            src_ref=source, dst_ref=target, send_sem=send_sem.at[number], recv_sem=recv_sem.at[number],
            device_id={"tp": device}, device_id_type=MESH,
        )
        copy.start()
        return copy

    def arrived(number, target):
        pltpu.make_async_remote_copy(
            src_ref=target, dst_ref=target, send_sem=send_sem.at[number], recv_sem=recv_sem.at[number],
            device_id={"tp": other}, device_id_type=MESH,
        ).wait_recv()

    sent = [
        send(0, grad_hbm.at[0:half], rows(tp, 0), right),
        send(2, grad_hbm.at[half:BLOCK], rows(tp, 1), left),
        send(6, grad_hbm, gall.at[pl.ds(pl.multiple_of(tp * BLOCK, BLOCK), BLOCK)], other),
        send(1, grad_hbm.at[half:BLOCK], rows(tp, 1), right),
        send(3, grad_hbm.at[0:half], rows(tp, 0), left),
    ]

    loads[3].wait()
    depth = tok.shape[0]
    for at_row in range(0, depth, 256):
        tok_t[:, at_row : at_row + 256] = tok[at_row : at_row + 256, :].T
    loads[2].wait()
    loads[4].wait()

    arrived(0, rows(left, 0))
    sent.append(send(4, rows(left, 0), rows(left, 0), right))
    sent.append(send(7, rows(left, 0), rows(left, 0), other))
    arrived(2, rows(right, 1))
    sent.append(send(5, rows(right, 1), rows(right, 1), left))
    sent.append(send(10, rows(right, 1), rows(right, 1), other))
    arrived(1, rows(left, 1))
    sent.append(send(8, rows(left, 1), rows(left, 1), other))
    arrived(3, rows(right, 0))
    sent.append(send(9, rows(right, 0), rows(right, 0), other))

    def forward(strip):
        grads = gall[pl.ds(pl.multiple_of(strip * LANES, LANES), LANES), :]
        gradient = lax.dot_general(tok_t[...], grads, NT, preferred_element_type=jnp.float32)
        moment = momentum_decay * mom[:, strip_of(strip)] + gradient
        mom[:, strip_of(strip)] = moment
        for p in range(rows_p):
            block = moment[p * BLOCK : (p + 1) * BLOCK]
            kept[strip * rows_p + p] = encode(block, at[p, :, strip_of(strip)], w[p, strip])

    def backward(strip):
        for p in range(rows_p):
            field = decode(kept[strip * rows_p + p], at[p, :, strip_of(strip)], w[p, strip])
            mom[p * BLOCK : (p + 1) * BLOCK, strip_of(strip)] = (
                mom[p * BLOCK : (p + 1) * BLOCK, strip_of(strip)] - field
            )

    left_x, right_x, far_x = lax.rem(x + NX - 1, NX), lax.rem(x + 1, NX), lax.rem(x + 2, NX)
    left_o, right_o, far_o = left_x * 2 + 1 - core, right_x * 2 + 1 - core, far_x * 2 + 1 - core

    arrived(6, gall.at[pl.ds(pl.multiple_of(other * BLOCK, BLOCK), BLOCK)])
    forward(x)
    arrived(7, rows(left_o, 0))
    arrived(8, rows(left_o, 1))
    forward(left_x)
    arrived(4, rows(far, 0))
    sent.append(send(11, rows(far, 0), rows(far, 0), other))
    arrived(5, rows(far, 1))
    sent.append(send(12, rows(far, 1), rows(far, 1), other))
    arrived(9, rows(right_o, 0))
    arrived(10, rows(right_o, 1))
    forward(right_x)
    arrived(11, rows(far_o, 0))
    arrived(12, rows(far_o, 1))
    forward(far_x)

    def scatter_z(step, carry):
        peer = lax.rem(z + step, nz)
        pltpu.make_async_remote_copy(
            src_ref=kept.at[pl.ds(peer * chunk, chunk)], dst_ref=part.at[z], send_sem=z_send.at[0], recv_sem=z_recv.at[0],
            device_id={"rep": peer * ny + y}, device_id_type=MESH,
        ).start()
        return carry

    lax.fori_loop(1, nz, scatter_z, 0)
    part[z] = kept[pl.ds(z * chunk, chunk)]
    backward(x)
    backward(left_x)
    many = part.at[pl.ds(0, nz - 1)]
    pltpu.make_async_copy(many, many, z_recv.at[0]).wait()
    ybuf[y] = jnp.sum(part[...], axis=0)

    def swap_y(step, carry):
        peer = z * ny + lax.rem(y + step, ny)
        pltpu.make_async_remote_copy(
            src_ref=ybuf.at[y], dst_ref=ybuf.at[y], send_sem=y_send, recv_sem=y_recv,
            device_id={"rep": peer}, device_id_type=MESH,
        ).start()
        return carry

    lax.fori_loop(1, ny, swap_y, 0)
    some = ybuf.at[pl.ds(0, ny - 1)]
    pltpu.make_async_copy(some, some, y_recv).wait()
    total[z] = jnp.sum(ybuf[...], axis=0)

    def gather_z(step, carry):
        peer = lax.rem(z + step, nz)
        pltpu.make_async_remote_copy(
            src_ref=total.at[z], dst_ref=total.at[z], send_sem=z_send.at[1], recv_sem=z_recv.at[1],
            device_id={"rep": peer * ny + y}, device_id_type=MESH,
        ).start()
        return carry

    lax.fori_loop(1, nz, gather_z, 0)
    backward(right_x)
    backward(far_x)
    res_out = pltpu.make_async_copy(mom, res_hbm, out_sem.at[2])
    res_out.start()
    most = total.at[pl.ds(0, nz - 1)]
    pltpu.make_async_copy(most, most, z_recv.at[1]).wait()
    total_out = pltpu.make_async_copy(total, total_hbm, out_sem.at[3])
    total_out.start()

    for copy in sent:
        copy.wait_send()
    pltpu.make_async_copy(many, many, z_send.at[0]).wait()
    pltpu.make_async_copy(some, some, y_send).wait()
    pltpu.make_async_copy(most, most, z_send.at[1]).wait()
    for copy in bases_out:
        copy.wait()
    res_out.wait()
    total_out.wait()


def second_kernel(
    total_hbm, at_hbm, w_hbm, res_in, weight_hbm, target_hbm,
    update_hbm, res_hbm, blended_hbm,
    total, at, w, weight, target, update, blended, load_sem, out_sem,
):
    res_copy = pltpu.make_async_copy(res_in, res_hbm, out_sem.at[0])
    loads = [
        pltpu.make_async_copy(total_hbm, total, load_sem.at[0]),
        pltpu.make_async_copy(at_hbm, at, load_sem.at[1]),
        pltpu.make_async_copy(w_hbm, w, load_sem.at[2]),
        pltpu.make_async_copy(weight_hbm, weight, load_sem.at[3]),
        pltpu.make_async_copy(target_hbm, target, load_sem.at[4]),
    ]
    for load in loads:
        load.start()
    res_copy.start()
    for load in loads:
        load.wait()
    rows_p, strips = w.shape[:2]
    outs = []
    for p in range(rows_p):
        at_rows = slice(p * BLOCK, (p + 1) * BLOCK)
        for g in range(strips):
            at_lanes = slice(g * LANES, (g + 1) * LANES)
            field = decode(total[g * rows_p + p], at[p, :, at_lanes], w[p, g])
            update[at_rows, at_lanes] = field
            moved = weight[at_rows, at_lanes].astype(jnp.float32) - update_rate * field
            mixed = (1.0 - polyak_rate) * target[at_rows, at_lanes].astype(jnp.float32) + polyak_rate * moved
            blended[at_rows, at_lanes] = mixed.astype(jnp.bfloat16)
        outs.append(pltpu.make_async_copy(update.at[at_rows], update_hbm.at[at_rows], out_sem.at[1 + 2 * p]))
        outs.append(pltpu.make_async_copy(blended.at[at_rows], blended_hbm.at[at_rows], out_sem.at[2 + 2 * p]))
        outs[-2].start()
        outs[-1].start()
    for copy in outs:
        copy.wait()
    res_copy.wait()


def shards(ny, nz, tokens, key_grad, momentum, key_weight, target, positions):
    anywhere = pl.BlockSpec(memory_space=pl.ANY)
    in_hbm = pl.BlockSpec(memory_space=pltpu.HBM)
    table = jnp.asarray(split_table())
    depth, feats = tokens.shape
    _, _, width = momentum.shape
    rows_p, col_blocks, keep = positions.shape
    strips = width // LANES
    rows = rows_p * strips
    chunk = rows // nz
    at_shape, w_shape = (rows_p, BLOCK, width), (rows_p, strips, 2 * BLOCK, 2 * LANES)
    residual, total, at, w = pl.pallas_call(
        functools.partial(first_kernel, ny, nz),
        out_shape=(
            jax.ShapeDtypeStruct((feats, width), jnp.float32),
            jax.ShapeDtypeStruct((nz, chunk, 1, LANES), jnp.float32),
            jax.ShapeDtypeStruct(at_shape, jnp.float32),
            jax.ShapeDtypeStruct(w_shape, jnp.bfloat16),
        ),
        in_specs=[in_hbm] * 5,
        out_specs=(anywhere,) * 4,
        scratch_shapes=[
            pltpu.VMEM((depth, feats), jnp.bfloat16),
            pltpu.VMEM((feats, depth), jnp.bfloat16),
            pltpu.VMEM((width, depth), jnp.bfloat16),
            pltpu.VMEM((feats, width), jnp.float32),
            pltpu.VMEM(at_shape, jnp.float32),
            pltpu.VMEM(w_shape, jnp.bfloat16),
            pltpu.VMEM((rows_p, col_blocks, keep), jnp.int32),
            pltpu.VMEM(table.shape, jnp.bfloat16),
            pltpu.VMEM((rows, 1, LANES), jnp.float32),
            pltpu.VMEM((nz, chunk, 1, LANES), jnp.float32),
            pltpu.VMEM((ny, chunk, 1, LANES), jnp.float32),
            pltpu.VMEM((nz, chunk, 1, LANES), jnp.float32),
            pltpu.SemaphoreType.DMA((5,)),
            pltpu.SemaphoreType.DMA((13,)),
            pltpu.SemaphoreType.DMA((13,)),
            pltpu.SemaphoreType.DMA((2,)),
            pltpu.SemaphoreType.DMA((2,)),
            pltpu.SemaphoreType.DMA,
            pltpu.SemaphoreType.DMA,
            pltpu.SemaphoreType.DMA((4,)),
        ],
        compiler_params=pltpu.CompilerParams(
            collective_id=0, has_side_effects=True, vmem_limit_bytes=32 * 1024 * 1024
        ),
        cost_estimate=pl.CostEstimate(flops=1_000_000_000, bytes_accessed=8_000_000, transcendentals=0),
        name="gather_encode_sum",
    )(tokens, key_grad.T, momentum[0], positions, table)
    update, residual, blended = pl.pallas_call(
        second_kernel,
        out_shape=(
            jax.ShapeDtypeStruct((feats, width), jnp.float32),
            jax.ShapeDtypeStruct((feats, width), jnp.float32),
            jax.ShapeDtypeStruct((feats, width), jnp.bfloat16),
        ),
        in_specs=[anywhere] * 6,
        out_specs=(anywhere,) * 3,
        scratch_shapes=[
            pltpu.VMEM((rows, 1, LANES), jnp.float32),
            pltpu.VMEM(at_shape, jnp.float32),
            pltpu.VMEM(w_shape, jnp.bfloat16),
            pltpu.VMEM((feats, width), jnp.bfloat16),
            pltpu.VMEM((feats, width), jnp.bfloat16),
            pltpu.VMEM((feats, width), jnp.float32),
            pltpu.VMEM((feats, width), jnp.bfloat16),
            pltpu.SemaphoreType.DMA((5,)),
            pltpu.SemaphoreType.DMA((1 + 2 * rows_p,)),
        ],
        compiler_params=pltpu.CompilerParams(vmem_limit_bytes=32 * 1024 * 1024),
        cost_estimate=pl.CostEstimate(flops=300_000_000, bytes_accessed=8_000_000, transcendentals=0),
        name="decode_blend",
    )(total.reshape(rows, 1, LANES), at, w, residual, key_weight, target)
    return (update, residual[None], blended)


def solution(mesh):
    in_specs = (
        P("rep", "tp"),
        P("rep", "tp"),
        P("rep", "tp", None),
        P("tp", None),
        P("tp", None),
        P("tp", None, None),
    )
    out_specs = (P("tp", None), P("rep", "tp", None), P("tp", None))
    body = functools.partial(shards, NY, mesh.shape["rep"] // NY)
    return jax.shard_map(body, mesh=mesh, in_specs=in_specs, out_specs=out_specs, check_vma=False)
```

```python
import functools

import jax
import jax.numpy as jnp
import ml_dtypes
import numpy as np
from jax import lax
from jax.experimental import pallas as pl
from jax.experimental.pallas import tpu as pltpu
from jax.sharding import PartitionSpec as P

BLOCK = 64
LANES = 128
NX, NY = 4, 4

momentum_decay = 0.9
polyak_rate = 0.25
update_rate = 0.1

MESH = pl.DeviceIdType.MESH
NT = (((1,), (1,)), ((), ()))


def split_table():
    index = np.arange(BLOCK, dtype=np.float64)
    angle = np.pi * (2.0 * index[:, None] + 1.0) * index[None, :] / (2.0 * BLOCK)
    scale = np.where(index == 0, np.sqrt(1.0 / BLOCK), np.sqrt(2.0 / BLOCK))
    table = np.cos(angle) * scale[None, :]
    high = table.astype(ml_dtypes.bfloat16)
    low = (table - high.astype(np.float64)).astype(ml_dtypes.bfloat16)
    return np.concatenate([high, low], axis=0)


def split_rows(value):
    high = value.astype(jnp.bfloat16)
    low = (value - high.astype(jnp.float32)).astype(jnp.bfloat16)
    return high, low


def strip_of(strip):
    return pl.ds(pl.multiple_of(strip * LANES, LANES), LANES)


def make_bases(pos_ref, table_ref, at_ref, w_ref):
    row_blocks, col_blocks, keep = pos_ref.shape
    width = col_blocks * keep
    lane = lax.broadcasted_iota(jnp.int32, (BLOCK, LANES), 1)
    level = lax.broadcasted_iota(jnp.int32, (BLOCK, width), 0)
    table = table_ref[...]
    flat = jnp.concatenate([pos_ref[:, b, :] for b in range(col_blocks)], axis=1)
    for p in range(row_blocks):
        row = flat[p : p + 1, :]
        first = jnp.where(level == (row >> 6), 1.0, 0.0).astype(jnp.bfloat16)
        second = jnp.where(level == (row & 63), 1.0, 0.0).astype(jnp.bfloat16)
        picked = jnp.dot(table, first, preferred_element_type=jnp.float32)
        at_ref[p] = picked[:BLOCK] + picked[BLOCK:]
        other = jnp.dot(table, second, preferred_element_type=jnp.float32)
        for g in range(width // LANES):
            for part in range(2):
                piece = other[part * BLOCK : (part + 1) * BLOCK, g * LANES : (g + 1) * LANES]
                top = jnp.where(lane < BLOCK, piece, 0.0).astype(jnp.bfloat16)
                low = jnp.where(lane < BLOCK, 0.0, piece).astype(jnp.bfloat16)
                w_ref[p, g, 0:BLOCK, part * LANES : (part + 1) * LANES] = top
                w_ref[p, g, BLOCK : 2 * BLOCK, part * LANES : (part + 1) * LANES] = low


def encode(block, at, w):
    high, low = split_rows(block)
    both = jnp.dot(jnp.concatenate([high, low], axis=0), w, preferred_element_type=jnp.float32)
    mixed = both[:BLOCK, :LANES] + both[:BLOCK, LANES:] + both[BLOCK:, :LANES]
    return jnp.sum(mixed * at, axis=0, keepdims=True)


def decode(values, at, w):
    high, low = split_rows(at * values)
    rows = jnp.concatenate(
        [jnp.concatenate([high, high], axis=1), jnp.concatenate([low, jnp.zeros_like(low)], axis=1)], axis=0
    )
    both = lax.dot_general(rows, w, NT, preferred_element_type=jnp.float32)
    return both[:BLOCK] + both[BLOCK:]


def first_kernel(
    ny, nz,
    tok_hbm, grad_hbm, mom_hbm, pos_hbm, table_hbm,
    res_out, total_out, at_out, w_out,
    tok, tok_t, gall, mom, at, w, pos, table, early, y_parts, z_parts, y_sums, total,
    load_sem, send_sem, recv_sem, sum_send, sum_recv, out_sem, know_y, know_z,
):
    rep, tp = lax.axis_index("rep"), lax.axis_index("tp")
    z, y = rep // ny, lax.rem(rep, ny)
    x, core = tp // 2, lax.rem(tp, 2)
    right = lax.rem(x + 1, NX) * 2 + core
    left = lax.rem(x + NX - 1, NX) * 2 + core
    far = lax.rem(x + 2, NX) * 2 + core
    other = 2 * x + 1 - core
    rows_p = at.shape[0]
    quarter = early.shape[0] // ny

    def z_peer(step):
        step = step % nz if isinstance(step, int) else step
        return {"rep": lax.rem(z + step + nz, nz) * ny + y}

    def y_peer(step):
        return {"rep": z * ny + lax.rem(y + step + ny, ny)}

    def tell(semaphore, device):
        pl.semaphore_signal(semaphore, inc=1, device_id=device, device_id_type=MESH)

    own_rows = gall.at[pl.ds(pl.multiple_of(tp * BLOCK, BLOCK), BLOCK)]
    loads = [
        pltpu.make_async_copy(pos_hbm, pos, load_sem.at[0]),
        pltpu.make_async_copy(table_hbm, table, load_sem.at[1]),
        pltpu.make_async_copy(grad_hbm, own_rows, load_sem.at[2]),
        pltpu.make_async_copy(tok_hbm, tok, load_sem.at[3]),
        pltpu.make_async_copy(mom_hbm, mom, load_sem.at[4]),
    ]

    barrier = pltpu.get_barrier_semaphore()
    for peer in (right, left, other):
        tell(barrier, {"tp": peer})
    for step in (1, -1):
        tell(barrier, z_peer(step))
        tell(barrier, y_peer(step))
    for load in loads:
        load.start()

    loads[0].wait()
    loads[1].wait()
    make_bases(pos, table, at, w)
    bases_out = [
        pltpu.make_async_copy(at, at_out, out_sem.at[0]),
        pltpu.make_async_copy(w, w_out, out_sem.at[1]),
    ]
    for copy in bases_out:
        copy.start()
    loads[2].wait()
    pl.semaphore_wait(barrier, 7)

    tell(know_y, y_peer(-1))
    tell(know_z.at[0], z_peer(1))
    tell(know_z.at[0], z_peer(-1))

    half = BLOCK // 2

    def rows(owner, part_at):
        return gall.at[pl.ds(pl.multiple_of(owner * BLOCK + part_at * half, half), half)]

    def send(number, block, device):
        copy = pltpu.make_async_remote_copy(
            src_ref=block, dst_ref=block, send_sem=send_sem.at[number], recv_sem=recv_sem.at[number],
            device_id={"tp": device}, device_id_type=MESH,
        )
        copy.start()
        return copy

    def arrived(number, block):
        pltpu.make_async_remote_copy(
            src_ref=block, dst_ref=block, send_sem=send_sem.at[number], recv_sem=recv_sem.at[number],
            device_id={"tp": other}, device_id_type=MESH,
        ).wait_recv()

    sent = [
        send(0, rows(tp, 0), right),
        send(2, rows(tp, 1), left),
        send(1, rows(tp, 1), right),
        send(3, rows(tp, 0), left),
        send(6, own_rows, other),
    ]

    loads[3].wait()
    depth = tok.shape[0]
    for at_row in range(0, depth, 256):
        tok_t[:, at_row : at_row + 256] = tok[at_row : at_row + 256, :].T
    loads[4].wait()

    pl.semaphore_wait(know_z.at[0], 2)
    tell(know_z.at[1], z_peer(2))
    tell(know_z.at[1], z_peer(-2))
    pl.semaphore_wait(know_y, 1)

    arrived(0, rows(left, 0))
    sent.append(send(4, rows(left, 0), right))
    arrived(2, rows(right, 1))
    sent.append(send(5, rows(right, 1), left))
    sent.append(send(7, rows(left, 0), other))
    sent.append(send(10, rows(right, 1), other))
    pl.semaphore_wait(know_z.at[1], 2)
    tell(know_z.at[2], z_peer(4))
    tell(know_z.at[2], z_peer(-4))
    arrived(1, rows(left, 1))
    sent.append(send(8, rows(left, 1), other))
    arrived(3, rows(right, 0))
    sent.append(send(9, rows(right, 0), other))

    def forward(strip, keep, base):
        grads = gall[pl.ds(pl.multiple_of(strip * LANES, LANES), LANES), :]
        gradient = lax.dot_general(tok_t[...], grads, NT, preferred_element_type=jnp.float32)
        moment = momentum_decay * mom[:, strip_of(strip)] + gradient
        mom[:, strip_of(strip)] = moment
        for p in range(rows_p):
            block = moment[p * BLOCK : (p + 1) * BLOCK]
            keep[base + p] = encode(block, at[p, :, strip_of(strip)], w[p, strip])

    def backward(strip, keep, base):
        for p in range(rows_p):
            field = decode(keep[base + p], at[p, :, strip_of(strip)], w[p, strip])
            mom[p * BLOCK : (p + 1) * BLOCK, strip_of(strip)] = (
                mom[p * BLOCK : (p + 1) * BLOCK, strip_of(strip)] - field
            )

    left_x, right_x, far_x = lax.rem(x + NX - 1, NX), lax.rem(x + 1, NX), lax.rem(x + 2, NX)
    left_o, right_o, far_o = left_x * 2 + 1 - core, right_x * 2 + 1 - core, far_x * 2 + 1 - core
    strips = (x, left_x, right_x, far_x)

    arrived(6, gall.at[pl.ds(pl.multiple_of(other * BLOCK, BLOCK), BLOCK)])
    forward(x, early, 0)
    arrived(7, rows(left_o, 0))
    arrived(8, rows(left_o, 1))
    forward(left_x, early, rows_p)
    pl.semaphore_wait(know_z.at[2], 2)
    tell(know_z.at[3], z_peer(8))
    tell(know_z.at[3], z_peer(-8))
    arrived(9, rows(right_o, 0))
    arrived(10, rows(right_o, 1))
    forward(right_x, early, 2 * rows_p)

    def early_y(step, carry):
        peer = lax.rem(y + step, ny)
        pltpu.make_async_remote_copy(
            src_ref=early.at[pl.ds(peer * quarter, quarter)], dst_ref=y_parts.at[y],
            send_sem=sum_send.at[0], recv_sem=sum_recv.at[0], device_id=y_peer(step), device_id_type=MESH,
        ).start()
        return carry

    lax.fori_loop(1, ny, early_y, 0)
    y_parts[y] = early[pl.ds(y * quarter, quarter)]

    arrived(4, rows(far, 0))
    sent.append(send(11, rows(far, 0), other))
    arrived(5, rows(far, 1))
    sent.append(send(12, rows(far, 1), other))
    arrived(11, rows(far_o, 0))
    arrived(12, rows(far_o, 1))
    mine = z_parts.at[z]
    forward(far_x, mine, quarter)

    three = y_parts.at[pl.ds(0, ny - 1)]
    pltpu.make_async_copy(three, three, sum_recv.at[0]).wait()
    mine[0:quarter] = jnp.sum(y_parts[...], axis=0)
    pl.semaphore_wait(know_z.at[3], 2)

    def across(step):
        pltpu.make_async_remote_copy(
            src_ref=mine, dst_ref=mine, send_sem=sum_send.at[1], recv_sem=sum_recv.at[1],
            device_id=z_peer(step), device_id_type=MESH,
        ).start()

    def both_ways(step, carry):
        across(nz // 2 - step)
        across(step - nz // 2)
        return carry

    across(nz // 2)
    lax.fori_loop(1, nz // 2, both_ways, 0)
    for number, strip in enumerate(strips[:3]):
        backward(strip, early, number * rows_p)
    backward(far_x, mine, quarter)
    res_copy = pltpu.make_async_copy(mom, res_out, out_sem.at[2])
    res_copy.start()
    many = z_parts.at[pl.ds(0, nz - 1)]
    pltpu.make_async_copy(many, many, sum_recv.at[1]).wait()
    y_sums[y] = jnp.sum(z_parts[...], axis=0)

    def late_y(step, carry):
        pltpu.make_async_remote_copy(
            src_ref=y_sums.at[y], dst_ref=y_sums.at[y], send_sem=sum_send.at[2], recv_sem=sum_recv.at[2],
            device_id=y_peer(step), device_id_type=MESH,
        ).start()
        return carry

    lax.fori_loop(1, ny, late_y, 0)
    some = y_sums.at[pl.ds(0, ny - 1)]
    pltpu.make_async_copy(some, some, sum_recv.at[2]).wait()
    for number, strip in enumerate(strips[:3]):
        for p in range(rows_p):
            row = number * rows_p + p
            total[strip * rows_p + p] = y_sums[row // quarter, row % quarter]
    last = jnp.sum(y_sums[:, quarter:], axis=0)
    for p in range(rows_p):
        total[far_x * rows_p + p] = last[p]
    total_copy = pltpu.make_async_copy(total, total_out, out_sem.at[3])
    total_copy.start()

    for copy in sent:
        copy.wait_send()
    pltpu.make_async_copy(three, three, sum_send.at[0]).wait()
    pltpu.make_async_copy(many, many, sum_send.at[1]).wait()
    pltpu.make_async_copy(some, some, sum_send.at[2]).wait()
    for copy in bases_out:
        copy.wait()
    res_copy.wait()
    total_copy.wait()


def second_kernel(
    total, at, w, res_in, weight, target,
    update_hbm, res_hbm, blended_hbm,
    update, blended, out_sem,
):
    res_copy = pltpu.make_async_copy(res_in, res_hbm, out_sem.at[0])
    res_copy.start()
    rows_p, strips = w.shape[:2]
    outs = []
    for p in range(rows_p):
        at_rows = slice(p * BLOCK, (p + 1) * BLOCK)
        for g in range(strips):
            at_lanes = slice(g * LANES, (g + 1) * LANES)
            field = decode(total[g * rows_p + p], at[p, :, at_lanes], w[p, g])
            update[at_rows, at_lanes] = field
            moved = weight[at_rows, at_lanes].astype(jnp.float32) - update_rate * field
            mixed = (1.0 - polyak_rate) * target[at_rows, at_lanes].astype(jnp.float32) + polyak_rate * moved
            blended[at_rows, at_lanes] = mixed.astype(jnp.bfloat16)
        outs.append(pltpu.make_async_copy(update.at[at_rows], update_hbm.at[at_rows], out_sem.at[1 + 2 * p]))
        outs.append(pltpu.make_async_copy(blended.at[at_rows], blended_hbm.at[at_rows], out_sem.at[2 + 2 * p]))
        outs[-2].start()
        outs[-1].start()
    for copy in outs:
        copy.wait()
    res_copy.wait()


def shards(ny, nz, tokens, key_grad, momentum, key_weight, target, positions):
    anywhere = pl.BlockSpec(memory_space=pl.ANY)
    table = jnp.asarray(split_table())
    depth, feats = tokens.shape
    _, _, width = momentum.shape
    rows_p, col_blocks, keep = positions.shape
    strips = width // LANES
    rows = rows_p * strips
    at_shape, w_shape = (rows_p, BLOCK, width), (rows_p, strips, 2 * BLOCK, 2 * LANES)
    early = (strips - 1) * rows_p
    quarter = early // ny
    residual, total, at, w = pl.pallas_call(
        functools.partial(first_kernel, ny, nz),
        out_shape=(
            pltpu.VMEM((feats, width), jnp.float32),
            pltpu.VMEM((rows, 1, LANES), jnp.float32),
            pltpu.VMEM(at_shape, jnp.float32),
            pltpu.VMEM(w_shape, jnp.bfloat16),
        ),
        in_specs=[anywhere] * 5,
        out_specs=(anywhere,) * 4,
        scratch_shapes=[
            pltpu.VMEM((depth, feats), jnp.bfloat16),
            pltpu.VMEM((feats, depth), jnp.bfloat16),
            pltpu.VMEM((width, depth), jnp.bfloat16),
            pltpu.VMEM((feats, width), jnp.float32),
            pltpu.VMEM(at_shape, jnp.float32),
            pltpu.VMEM(w_shape, jnp.bfloat16),
            pltpu.VMEM((rows_p, col_blocks, keep), jnp.int32),
            pltpu.VMEM(table.shape, jnp.bfloat16),
            pltpu.VMEM((early, 1, LANES), jnp.float32),
            pltpu.VMEM((ny, quarter, 1, LANES), jnp.float32),
            pltpu.VMEM((nz, quarter + rows_p, 1, LANES), jnp.float32),
            pltpu.VMEM((ny, quarter + rows_p, 1, LANES), jnp.float32),
            pltpu.VMEM((rows, 1, LANES), jnp.float32),
            pltpu.SemaphoreType.DMA((5,)),
            pltpu.SemaphoreType.DMA((13,)),
            pltpu.SemaphoreType.DMA((13,)),
            pltpu.SemaphoreType.DMA((3,)),
            pltpu.SemaphoreType.DMA((3,)),
            pltpu.SemaphoreType.DMA((4,)),
            pltpu.SemaphoreType.REGULAR,
            pltpu.SemaphoreType.REGULAR((4,)),
        ],
        compiler_params=pltpu.CompilerParams(
            collective_id=0, has_side_effects=True, vmem_limit_bytes=54 * 1024 * 1024
        ),
        cost_estimate=pl.CostEstimate(flops=1_000_000_000, bytes_accessed=8_000_000, transcendentals=0),
        name="gather_encode_sum",
    )(tokens, key_grad.T, momentum[0], positions, table)
    in_vmem = pl.BlockSpec(memory_space=pltpu.VMEM)
    update, residual, blended = pl.pallas_call(
        second_kernel,
        out_shape=(
            jax.ShapeDtypeStruct((feats, width), jnp.float32),
            jax.ShapeDtypeStruct((feats, width), jnp.float32),
            jax.ShapeDtypeStruct((feats, width), jnp.bfloat16),
        ),
        in_specs=[in_vmem] * 3 + [anywhere] + [in_vmem] * 2,
        out_specs=(anywhere,) * 3,
        scratch_shapes=[
            pltpu.VMEM((feats, width), jnp.float32),
            pltpu.VMEM((feats, width), jnp.bfloat16),
            pltpu.SemaphoreType.DMA((1 + 2 * rows_p,)),
        ],
        compiler_params=pltpu.CompilerParams(vmem_limit_bytes=32 * 1024 * 1024),
        cost_estimate=pl.CostEstimate(flops=300_000_000, bytes_accessed=8_000_000, transcendentals=0),
        name="decode_blend",
    )(total, at, w, residual, key_weight, target)
    return (update, residual[None], blended)


def solution(mesh):
    in_specs = (
        P("rep", "tp"),
        P("rep", "tp"),
        P("rep", "tp", None),
        P("tp", None),
        P("tp", None),
        P("tp", None, None),
    )
    out_specs = (P("tp", None), P("rep", "tp", None), P("tp", None))
    body = functools.partial(shards, NY, mesh.shape["rep"] // NY)
    return jax.shard_map(body, mesh=mesh, in_specs=in_specs, out_specs=out_specs, check_vma=False)
```

```python
import functools

import jax
import jax.numpy as jnp
import ml_dtypes
import numpy as np
from jax import lax
from jax.experimental import pallas as pl
from jax.experimental.pallas import tpu as pltpu
from jax.sharding import PartitionSpec as P

BLOCK = 64
LANES = 128
NX, NY = 4, 4

momentum_decay = 0.9
polyak_rate = 0.25
update_rate = 0.1

MESH = pl.DeviceIdType.MESH
NT = (((1,), (1,)), ((), ()))


def split_table():
    index = np.arange(BLOCK, dtype=np.float64)
    angle = np.pi * (2.0 * index[:, None] + 1.0) * index[None, :] / (2.0 * BLOCK)
    scale = np.where(index == 0, np.sqrt(1.0 / BLOCK), np.sqrt(2.0 / BLOCK))
    table = np.cos(angle) * scale[None, :]
    high = table.astype(ml_dtypes.bfloat16)
    low = (table - high.astype(np.float64)).astype(ml_dtypes.bfloat16)
    return np.concatenate([high, low], axis=0)


def split_rows(value):
    high = value.astype(jnp.bfloat16)
    low = (value - high.astype(jnp.float32)).astype(jnp.bfloat16)
    return high, low


def strip_of(strip):
    return pl.ds(pl.multiple_of(strip * LANES, LANES), LANES)


def make_bases(pos_ref, table_ref, at_ref, w_ref):
    row_blocks, col_blocks, keep = pos_ref.shape
    width = col_blocks * keep
    lane = lax.broadcasted_iota(jnp.int32, (BLOCK, LANES), 1)
    level = lax.broadcasted_iota(jnp.int32, (BLOCK, width), 0)
    table = table_ref[...]
    flat = jnp.concatenate([pos_ref[:, b, :] for b in range(col_blocks)], axis=1)
    for p in range(row_blocks):
        row = flat[p : p + 1, :]
        first = jnp.where(level == (row >> 6), 1.0, 0.0).astype(jnp.bfloat16)
        second = jnp.where(level == (row & 63), 1.0, 0.0).astype(jnp.bfloat16)
        picked = jnp.dot(table, first, preferred_element_type=jnp.float32)
        at_ref[p] = picked[:BLOCK] + picked[BLOCK:]
        other = jnp.dot(table, second, preferred_element_type=jnp.float32)
        for g in range(width // LANES):
            for part in range(2):
                piece = other[part * BLOCK : (part + 1) * BLOCK, g * LANES : (g + 1) * LANES]
                top = jnp.where(lane < BLOCK, piece, 0.0).astype(jnp.bfloat16)
                low = jnp.where(lane < BLOCK, 0.0, piece).astype(jnp.bfloat16)
                w_ref[p, g, 0:BLOCK, part * LANES : (part + 1) * LANES] = top
                w_ref[p, g, BLOCK : 2 * BLOCK, part * LANES : (part + 1) * LANES] = low


def encode(block, at, w):
    high, low = split_rows(block)
    both = jnp.dot(jnp.concatenate([high, low], axis=0), w, preferred_element_type=jnp.float32)
    mixed = both[:BLOCK, :LANES] + both[:BLOCK, LANES:] + both[BLOCK:, :LANES]
    return jnp.sum(mixed * at, axis=0, keepdims=True)


def decode(values, at, w):
    high, low = split_rows(at * values)
    rows = jnp.concatenate(
        [jnp.concatenate([high, high], axis=1), jnp.concatenate([low, jnp.zeros_like(low)], axis=1)], axis=0
    )
    both = lax.dot_general(rows, w, NT, preferred_element_type=jnp.float32)
    return both[:BLOCK] + both[BLOCK:]


def first_kernel(
    ny, nz,
    tok_hbm, grad_hbm, mom_hbm, pos_hbm, table_hbm,
    res_out, total_out, at_out, w_out,
    tok, tok_t, gall, mom, at, w, pos, table, early, late, y_parts, z_parts, y_sums, total,
    load_sem, send_sem, recv_sem, sum_send, sum_recv, out_sem, know_y, know_down, know_up,
):
    rep, tp = lax.axis_index("rep"), lax.axis_index("tp")
    z, y = rep // ny, lax.rem(rep, ny)
    x, core = tp // 2, lax.rem(tp, 2)
    right = lax.rem(x + 1, NX) * 2 + core
    left = lax.rem(x + NX - 1, NX) * 2 + core
    far = lax.rem(x + 2, NX) * 2 + core
    other = 2 * x + 1 - core
    rows_p = at.shape[0]
    quarter = early.shape[0] // ny

    def z_peer(step):
        step = step % nz if isinstance(step, int) else step
        return {"rep": lax.rem(z + step + nz, nz) * ny + y}

    def y_peer(step):
        return {"rep": z * ny + lax.rem(y + step + ny, ny)}

    def tell(semaphore, device):
        pl.semaphore_signal(semaphore, inc=1, device_id=device, device_id_type=MESH)

    own_rows = gall.at[pl.ds(pl.multiple_of(tp * BLOCK, BLOCK), BLOCK)]
    loads = [
        pltpu.make_async_copy(pos_hbm, pos, load_sem.at[0]),
        pltpu.make_async_copy(table_hbm, table, load_sem.at[1]),
        pltpu.make_async_copy(grad_hbm, own_rows, load_sem.at[2]),
        pltpu.make_async_copy(tok_hbm, tok, load_sem.at[3]),
        pltpu.make_async_copy(mom_hbm, mom, load_sem.at[4]),
    ]

    loads[2].start()
    barrier = pltpu.get_barrier_semaphore()
    for peer in (right, left, other):
        tell(barrier, {"tp": peer})
    for step in (1, -1):
        tell(barrier, z_peer(step))
        tell(barrier, y_peer(step))
    for number in (3, 4, 0, 1):
        loads[number].start()

    loads[2].wait()
    pl.semaphore_wait(barrier, 7)

    half = BLOCK // 2

    def rows(owner, part_at):
        return gall.at[pl.ds(pl.multiple_of(owner * BLOCK + part_at * half, half), half)]

    def send(number, block, device):
        copy = pltpu.make_async_remote_copy(
            src_ref=block, dst_ref=block, send_sem=send_sem.at[number], recv_sem=recv_sem.at[number],
            device_id={"tp": device}, device_id_type=MESH,
        )
        copy.start()
        return copy

    def arrived(number, block):
        pltpu.make_async_remote_copy(
            src_ref=block, dst_ref=block, send_sem=send_sem.at[number], recv_sem=recv_sem.at[number],
            device_id={"tp": other}, device_id_type=MESH,
        ).wait_recv()

    sent = [
        send(0, rows(tp, 0), right),
        send(2, rows(tp, 1), left),
        send(1, rows(tp, 1), right),
        send(3, rows(tp, 0), left),
        send(6, own_rows, other),
    ]

    def pass_on(level):
        tell(know_down.at[level], z_peer(1 << level))
        tell(know_up.at[level], z_peer(-(1 << level)))

    def learn(level):
        pl.semaphore_wait(know_down.at[level], 1)
        pl.semaphore_wait(know_up.at[level], 1)
        if level + 1 < levels:
            pass_on(level + 1)

    levels = know_down.shape[0]
    tell(know_y, y_peer(-1))
    pass_on(0)

    loads[3].wait()
    depth = tok.shape[0]
    for at_row in range(0, depth, 256):
        tok_t[:, at_row : at_row + 256] = tok[at_row : at_row + 256, :].T
    loads[4].wait()
    pl.semaphore_wait(know_y, 1)
    learn(0)
    loads[0].wait()
    loads[1].wait()
    make_bases(pos, table, at, w)
    bases_out = [
        pltpu.make_async_copy(at, at_out, out_sem.at[0]),
        pltpu.make_async_copy(w, w_out, out_sem.at[1]),
    ]
    for copy in bases_out:
        copy.start()
    learn(1)

    arrived(0, rows(left, 0))
    sent.append(send(4, rows(left, 0), right))
    arrived(2, rows(right, 1))
    sent.append(send(5, rows(right, 1), left))
    sent.append(send(7, rows(left, 0), other))
    sent.append(send(10, rows(right, 1), other))
    arrived(1, rows(left, 1))
    sent.append(send(8, rows(left, 1), other))
    arrived(3, rows(right, 0))
    sent.append(send(9, rows(right, 0), other))

    def forward(strip, keep, base):
        grads = gall[pl.ds(pl.multiple_of(strip * LANES, LANES), LANES), :]
        gradient = lax.dot_general(tok_t[...], grads, NT, preferred_element_type=jnp.float32)
        moment = momentum_decay * mom[:, strip_of(strip)] + gradient
        mom[:, strip_of(strip)] = moment
        for p in range(rows_p):
            block = moment[p * BLOCK : (p + 1) * BLOCK]
            keep[base + p] = encode(block, at[p, :, strip_of(strip)], w[p, strip])

    def backward(strip, keep, base):
        for p in range(rows_p):
            field = decode(keep[base + p], at[p, :, strip_of(strip)], w[p, strip])
            mom[p * BLOCK : (p + 1) * BLOCK, strip_of(strip)] = (
                mom[p * BLOCK : (p + 1) * BLOCK, strip_of(strip)] - field
            )

    left_x, right_x, far_x = lax.rem(x + NX - 1, NX), lax.rem(x + 1, NX), lax.rem(x + 2, NX)
    left_o, right_o, far_o = left_x * 2 + 1 - core, right_x * 2 + 1 - core, far_x * 2 + 1 - core
    strips = (x, left_x, right_x, far_x)

    arrived(6, gall.at[pl.ds(pl.multiple_of(other * BLOCK, BLOCK), BLOCK)])
    forward(x, early, 0)
    arrived(7, rows(left_o, 0))
    arrived(8, rows(left_o, 1))
    forward(left_x, early, rows_p)
    for level in range(2, levels - 1):
        learn(level)
    arrived(9, rows(right_o, 0))
    arrived(10, rows(right_o, 1))
    forward(right_x, early, 2 * rows_p)

    def early_y(step, carry):
        peer = lax.rem(y + step, ny)
        pltpu.make_async_remote_copy(
            src_ref=early.at[pl.ds(peer * quarter, quarter)], dst_ref=y_parts.at[y],
            send_sem=sum_send.at[0], recv_sem=sum_recv.at[0], device_id=y_peer(step), device_id_type=MESH,
        ).start()
        return carry

    lax.fori_loop(1, ny, early_y, 0)
    y_parts[y] = early[pl.ds(y * quarter, quarter)]

    arrived(4, rows(far, 0))
    sent.append(send(11, rows(far, 0), other))
    arrived(5, rows(far, 1))
    sent.append(send(12, rows(far, 1), other))
    arrived(11, rows(far_o, 0))
    arrived(12, rows(far_o, 1))
    forward(far_x, late, 0)

    three = y_parts.at[pl.ds(0, ny - 1)]
    pltpu.make_async_copy(three, three, sum_recv.at[0]).wait()
    firsts = jnp.sum(y_parts[...], axis=0)
    rest = jnp.zeros((z_parts.shape[1] - quarter - rows_p, LANES), jnp.float32)
    mine = [firsts[row] for row in range(quarter)] + [late[p] for p in range(rows_p)] + [rest]
    z_parts[z] = jnp.concatenate(mine, axis=0).astype(jnp.bfloat16)
    learn(levels - 1)

    def across(step):
        pltpu.make_async_remote_copy(
            src_ref=z_parts.at[z], dst_ref=z_parts.at[z], send_sem=sum_send.at[1], recv_sem=sum_recv.at[1],
            device_id=z_peer(step), device_id_type=MESH,
        ).start()

    def both_ways(step, carry):
        across(nz // 2 - step)
        across(step - nz // 2)
        return carry

    across(nz // 2)
    lax.fori_loop(1, nz // 2, both_ways, 0)
    for number, strip in enumerate(strips[:3]):
        backward(strip, early, number * rows_p)
    backward(far_x, late, 0)
    res_copy = pltpu.make_async_copy(mom, res_out, out_sem.at[2])
    res_copy.start()
    many = z_parts.at[pl.ds(0, nz - 1)]
    pltpu.make_async_copy(many, many, sum_recv.at[1]).wait()
    y_sums[y] = jnp.sum(z_parts[...].astype(jnp.float32), axis=0)

    def late_y(step, carry):
        pltpu.make_async_remote_copy(
            src_ref=y_sums.at[y], dst_ref=y_sums.at[y], send_sem=sum_send.at[2], recv_sem=sum_recv.at[2],
            device_id=y_peer(step), device_id_type=MESH,
        ).start()
        return carry

    lax.fori_loop(1, ny, late_y, 0)
    some = y_sums.at[pl.ds(0, ny - 1)]
    pltpu.make_async_copy(some, some, sum_recv.at[2]).wait()
    for number, strip in enumerate(strips[:3]):
        for p in range(rows_p):
            row = number * rows_p + p
            at_row = row % quarter
            total[strip * rows_p + p] = y_sums[row // quarter, at_row : at_row + 1]
    last = jnp.sum(y_sums[...], axis=0)
    for p in range(rows_p):
        total[far_x * rows_p + p] = last[quarter + p : quarter + p + 1]
    total_copy = pltpu.make_async_copy(total, total_out, out_sem.at[3])
    total_copy.start()

    for copy in sent:
        copy.wait_send()
    pltpu.make_async_copy(three, three, sum_send.at[0]).wait()
    pltpu.make_async_copy(many, many, sum_send.at[1]).wait()
    pltpu.make_async_copy(some, some, sum_send.at[2]).wait()
    for copy in bases_out:
        copy.wait()
    res_copy.wait()
    total_copy.wait()


def second_kernel(
    total, at, w, res_in, weight, target,
    update_hbm, res_hbm, blended_hbm,
    update, blended, out_sem,
):
    res_copy = pltpu.make_async_copy(res_in, res_hbm, out_sem.at[0])
    res_copy.start()
    rows_p, strips = w.shape[:2]
    outs = []
    for p in range(rows_p):
        at_rows = slice(p * BLOCK, (p + 1) * BLOCK)
        for g in range(strips):
            at_lanes = slice(g * LANES, (g + 1) * LANES)
            field = decode(total[g * rows_p + p], at[p, :, at_lanes], w[p, g])
            update[at_rows, at_lanes] = field
            moved = weight[at_rows, at_lanes].astype(jnp.float32) - update_rate * field
            mixed = (1.0 - polyak_rate) * target[at_rows, at_lanes].astype(jnp.float32) + polyak_rate * moved
            blended[at_rows, at_lanes] = mixed.astype(jnp.bfloat16)
        outs.append(pltpu.make_async_copy(update.at[at_rows], update_hbm.at[at_rows], out_sem.at[1 + 2 * p]))
        outs.append(pltpu.make_async_copy(blended.at[at_rows], blended_hbm.at[at_rows], out_sem.at[2 + 2 * p]))
        outs[-2].start()
        outs[-1].start()
    for copy in outs:
        copy.wait()
    res_copy.wait()


def shards(ny, nz, tokens, key_grad, momentum, key_weight, target, positions):
    anywhere = pl.BlockSpec(memory_space=pl.ANY)
    table = jnp.asarray(split_table())
    depth, feats = tokens.shape
    _, _, width = momentum.shape
    rows_p, col_blocks, keep = positions.shape
    strips = width // LANES
    rows = rows_p * strips
    at_shape, w_shape = (rows_p, BLOCK, width), (rows_p, strips, 2 * BLOCK, 2 * LANES)
    early = (strips - 1) * rows_p
    quarter = early // ny
    residual, total, at, w = pl.pallas_call(
        functools.partial(first_kernel, ny, nz),
        out_shape=(
            pltpu.VMEM((feats, width), jnp.float32),
            pltpu.VMEM((rows, 1, LANES), jnp.float32),
            pltpu.VMEM(at_shape, jnp.float32),
            pltpu.VMEM(w_shape, jnp.bfloat16),
        ),
        in_specs=[anywhere] * 5,
        out_specs=(anywhere,) * 4,
        scratch_shapes=[
            pltpu.VMEM((depth, feats), jnp.bfloat16),
            pltpu.VMEM((feats, depth), jnp.bfloat16),
            pltpu.VMEM((width, depth), jnp.bfloat16),
            pltpu.VMEM((feats, width), jnp.float32),
            pltpu.VMEM(at_shape, jnp.float32),
            pltpu.VMEM(w_shape, jnp.bfloat16),
            pltpu.VMEM((rows_p, col_blocks, keep), jnp.int32),
            pltpu.VMEM(table.shape, jnp.bfloat16),
            pltpu.VMEM((early, 1, LANES), jnp.float32),
            pltpu.VMEM((rows_p, 1, LANES), jnp.float32),
            pltpu.VMEM((ny, quarter, 1, LANES), jnp.float32),
            pltpu.VMEM((nz, 16, LANES), jnp.bfloat16),
            pltpu.VMEM((ny, 16, LANES), jnp.float32),
            pltpu.VMEM((rows, 1, LANES), jnp.float32),
            pltpu.SemaphoreType.DMA((5,)),
            pltpu.SemaphoreType.DMA((13,)),
            pltpu.SemaphoreType.DMA((13,)),
            pltpu.SemaphoreType.DMA((3,)),
            pltpu.SemaphoreType.DMA((3,)),
            pltpu.SemaphoreType.DMA((4,)),
            pltpu.SemaphoreType.REGULAR,
            pltpu.SemaphoreType.REGULAR(((nz // 2).bit_length() - 1,)),
            pltpu.SemaphoreType.REGULAR(((nz // 2).bit_length() - 1,)),
        ],
        compiler_params=pltpu.CompilerParams(
            collective_id=0, has_side_effects=True, vmem_limit_bytes=54 * 1024 * 1024
        ),
        cost_estimate=pl.CostEstimate(flops=1_000_000_000, bytes_accessed=8_000_000, transcendentals=0),
        name="gather_encode_sum",
    )(tokens, key_grad.T, momentum[0], positions, table)
    in_vmem = pl.BlockSpec(memory_space=pltpu.VMEM)
    update, residual, blended = pl.pallas_call(
        second_kernel,
        out_shape=(
            jax.ShapeDtypeStruct((feats, width), jnp.float32),
            jax.ShapeDtypeStruct((feats, width), jnp.float32),
            jax.ShapeDtypeStruct((feats, width), jnp.bfloat16),
        ),
        in_specs=[in_vmem] * 3 + [anywhere] + [in_vmem] * 2,
        out_specs=(anywhere,) * 3,
        scratch_shapes=[
            pltpu.VMEM((feats, width), jnp.float32),
            pltpu.VMEM((feats, width), jnp.bfloat16),
            pltpu.SemaphoreType.DMA((1 + 2 * rows_p,)),
        ],
        compiler_params=pltpu.CompilerParams(vmem_limit_bytes=32 * 1024 * 1024),
        cost_estimate=pl.CostEstimate(flops=300_000_000, bytes_accessed=8_000_000, transcendentals=0),
        name="decode_blend",
    )(total, at, w, residual, key_weight, target)
    return (update, residual[None], blended)


def solution(mesh):
    in_specs = (
        P("rep", "tp"),
        P("rep", "tp"),
        P("rep", "tp", None),
        P("tp", None),
        P("tp", None),
        P("tp", None, None),
    )
    out_specs = (P("tp", None), P("rep", "tp", None), P("tp", None))
    body = functools.partial(shards, NY, mesh.shape["rep"] // NY)
    return jax.shard_map(body, mesh=mesh, in_specs=in_specs, out_specs=out_specs, check_vma=False)
```

```python
import functools

import jax
import jax.numpy as jnp
import ml_dtypes
import numpy as np
from jax import lax
from jax.experimental import pallas as pl
from jax.experimental.pallas import tpu as pltpu
from jax.sharding import PartitionSpec as P

BLOCK = 64
LANES = 128
NX, NY = 4, 4

momentum_decay = 0.9
polyak_rate = 0.25
update_rate = 0.1

MESH = pl.DeviceIdType.MESH
NT = (((1,), (1,)), ((), ()))


def split_table():
    index = np.arange(BLOCK, dtype=np.float64)
    angle = np.pi * (2.0 * index[:, None] + 1.0) * index[None, :] / (2.0 * BLOCK)
    scale = np.where(index == 0, np.sqrt(1.0 / BLOCK), np.sqrt(2.0 / BLOCK))
    table = np.cos(angle) * scale[None, :]
    high = table.astype(ml_dtypes.bfloat16)
    low = (table - high.astype(np.float64)).astype(ml_dtypes.bfloat16)
    return np.concatenate([high, low], axis=0)


def split_rows(value):
    high = value.astype(jnp.bfloat16)
    low = (value - high.astype(jnp.float32)).astype(jnp.bfloat16)
    return high, low


def strip_of(strip):
    return pl.ds(pl.multiple_of(strip * LANES, LANES), LANES)


def make_bases(pos_ref, table_ref, at_ref, w_ref):
    row_blocks, col_blocks, keep = pos_ref.shape
    width = col_blocks * keep
    lane = lax.broadcasted_iota(jnp.int32, (BLOCK, LANES), 1)
    level = lax.broadcasted_iota(jnp.int32, (BLOCK, width), 0)
    table = table_ref[...]
    flat = jnp.concatenate([pos_ref[:, b, :] for b in range(col_blocks)], axis=1)
    for p in range(row_blocks):
        row = flat[p : p + 1, :]
        first = jnp.where(level == (row >> 6), 1.0, 0.0).astype(jnp.bfloat16)
        second = jnp.where(level == (row & 63), 1.0, 0.0).astype(jnp.bfloat16)
        picked = jnp.dot(table, first, preferred_element_type=jnp.float32)
        at_ref[p] = picked[:BLOCK] + picked[BLOCK:]
        other = jnp.dot(table, second, preferred_element_type=jnp.float32)
        for g in range(width // LANES):
            for part in range(2):
                piece = other[part * BLOCK : (part + 1) * BLOCK, g * LANES : (g + 1) * LANES]
                top = jnp.where(lane < BLOCK, piece, 0.0).astype(jnp.bfloat16)
                low = jnp.where(lane < BLOCK, 0.0, piece).astype(jnp.bfloat16)
                w_ref[p, g, 0:BLOCK, part * LANES : (part + 1) * LANES] = top
                w_ref[p, g, BLOCK : 2 * BLOCK, part * LANES : (part + 1) * LANES] = low


def encode(block, at, w):
    high, low = split_rows(block)
    both = jnp.dot(jnp.concatenate([high, low], axis=0), w, preferred_element_type=jnp.float32)
    mixed = both[:BLOCK, :LANES] + both[:BLOCK, LANES:] + both[BLOCK:, :LANES]
    return jnp.sum(mixed * at, axis=0, keepdims=True)


def decode(values, at, w):
    high, low = split_rows(at * values)
    rows = jnp.concatenate(
        [jnp.concatenate([high, high], axis=1), jnp.concatenate([low, jnp.zeros_like(low)], axis=1)], axis=0
    )
    both = lax.dot_general(rows, w, NT, preferred_element_type=jnp.float32)
    return both[:BLOCK] + both[BLOCK:]


def first_kernel(
    ny, nz,
    tok_hbm, grad_hbm, mom_hbm, pos_hbm, table_hbm,
    res_out, total_out, at_out, w_out,
    tok, tok_t, gall, mom, at, w, pos, table, early, late, y_parts, z_parts, y_sums, total,
    load_sem, send_sem, recv_sem, sum_send, sum_recv, out_sem, know_down, know_up,
):
    rep, tp = lax.axis_index("rep"), lax.axis_index("tp")
    z, y = rep // ny, lax.rem(rep, ny)
    x, core = tp // 2, lax.rem(tp, 2)
    right = lax.rem(x + 1, NX) * 2 + core
    left = lax.rem(x + NX - 1, NX) * 2 + core
    far = lax.rem(x + 2, NX) * 2 + core
    other = 2 * x + 1 - core
    rows_p = at.shape[0]
    quarter = early.shape[0] // ny

    def z_peer(step):
        step = step % nz if isinstance(step, int) else step
        return {"rep": lax.rem(z + step + nz, nz) * ny + y}

    def y_peer(step):
        return {"rep": z * ny + lax.rem(y + step + ny, ny)}

    def tell(semaphore, device):
        pl.semaphore_signal(semaphore, inc=1, device_id=device, device_id_type=MESH)

    own_rows = gall.at[pl.ds(pl.multiple_of(tp * BLOCK, BLOCK), BLOCK)]
    loads = [
        pltpu.make_async_copy(pos_hbm, pos, load_sem.at[0]),
        pltpu.make_async_copy(table_hbm, table, load_sem.at[1]),
        pltpu.make_async_copy(grad_hbm, own_rows, load_sem.at[2]),
        pltpu.make_async_copy(tok_hbm, tok, load_sem.at[3]),
        pltpu.make_async_copy(mom_hbm, mom, load_sem.at[4]),
    ]

    loads[2].start()
    barrier = pltpu.get_barrier_semaphore()
    for peer in (right, left, other):
        tell(barrier, {"tp": peer})
    for step in (2, -2, 1, -1):
        tell(barrier, z_peer(step))
    for step in range(1, ny):
        tell(barrier, y_peer(step))
    for number in (3, 4, 0, 1):
        loads[number].start()

    loads[2].wait()
    pl.semaphore_wait(barrier, 3 + 4 + ny - 1)

    levels = know_down.shape[0]

    def pass_on(level):
        tell(know_down.at[level], z_peer(2 << level))
        tell(know_up.at[level], z_peer(-(2 << level)))

    def learn(level):
        pl.semaphore_wait(know_down.at[level], 1)
        pl.semaphore_wait(know_up.at[level], 1)
        if level + 1 < levels:
            pass_on(level + 1)

    pass_on(0)
    half = BLOCK // 2

    def rows(owner, part_at):
        return gall.at[pl.ds(pl.multiple_of(owner * BLOCK + part_at * half, half), half)]

    def send(number, block, device):
        copy = pltpu.make_async_remote_copy(
            src_ref=block, dst_ref=block, send_sem=send_sem.at[number], recv_sem=recv_sem.at[number],
            device_id={"tp": device}, device_id_type=MESH,
        )
        copy.start()
        return copy

    def arrived(number, block):
        pltpu.make_async_remote_copy(
            src_ref=block, dst_ref=block, send_sem=send_sem.at[number], recv_sem=recv_sem.at[number],
            device_id={"tp": other}, device_id_type=MESH,
        ).wait_recv()

    sent = [
        send(0, rows(tp, 0), right),
        send(2, rows(tp, 1), left),
        send(1, rows(tp, 1), right),
        send(3, rows(tp, 0), left),
        send(6, own_rows, other),
    ]

    loads[3].wait()
    depth = tok.shape[0]
    for at_row in range(0, depth, 256):
        tok_t[:, at_row : at_row + 256] = tok[at_row : at_row + 256, :].T
    loads[4].wait()
    loads[0].wait()
    loads[1].wait()
    make_bases(pos, table, at, w)
    bases_out = [
        pltpu.make_async_copy(at, at_out, out_sem.at[0]),
        pltpu.make_async_copy(w, w_out, out_sem.at[1]),
    ]
    for copy in bases_out:
        copy.start()
    learn(0)

    arrived(0, rows(left, 0))
    sent.append(send(4, rows(left, 0), right))
    arrived(2, rows(right, 1))
    sent.append(send(5, rows(right, 1), left))
    sent.append(send(7, rows(left, 0), other))
    sent.append(send(10, rows(right, 1), other))
    arrived(1, rows(left, 1))
    sent.append(send(8, rows(left, 1), other))
    arrived(3, rows(right, 0))
    sent.append(send(9, rows(right, 0), other))

    def forward(strip, keep, base):
        grads = gall[pl.ds(pl.multiple_of(strip * LANES, LANES), LANES), :]
        gradient = lax.dot_general(tok_t[...], grads, NT, preferred_element_type=jnp.float32)
        moment = momentum_decay * mom[:, strip_of(strip)] + gradient
        mom[:, strip_of(strip)] = moment
        for p in range(rows_p):
            block = moment[p * BLOCK : (p + 1) * BLOCK]
            keep[base + p] = encode(block, at[p, :, strip_of(strip)], w[p, strip])

    def backward(strip, keep, base):
        for p in range(rows_p):
            field = decode(keep[base + p], at[p, :, strip_of(strip)], w[p, strip])
            mom[p * BLOCK : (p + 1) * BLOCK, strip_of(strip)] = (
                mom[p * BLOCK : (p + 1) * BLOCK, strip_of(strip)] - field
            )

    left_x, right_x, far_x = lax.rem(x + NX - 1, NX), lax.rem(x + 1, NX), lax.rem(x + 2, NX)
    left_o, right_o, far_o = left_x * 2 + 1 - core, right_x * 2 + 1 - core, far_x * 2 + 1 - core
    strips = (x, left_x, right_x, far_x)

    arrived(6, gall.at[pl.ds(pl.multiple_of(other * BLOCK, BLOCK), BLOCK)])
    forward(x, early, 0)
    for level in range(1, levels - 1):
        learn(level)
    arrived(7, rows(left_o, 0))
    arrived(8, rows(left_o, 1))
    forward(left_x, early, rows_p)
    arrived(9, rows(right_o, 0))
    arrived(10, rows(right_o, 1))
    forward(right_x, early, 2 * rows_p)

    def early_y(step, carry):
        peer = lax.rem(y + step, ny)
        pltpu.make_async_remote_copy(
            src_ref=early.at[pl.ds(peer * quarter, quarter)], dst_ref=y_parts.at[y],
            send_sem=sum_send.at[0], recv_sem=sum_recv.at[0], device_id=y_peer(step), device_id_type=MESH,
        ).start()
        return carry

    lax.fori_loop(1, ny, early_y, 0)
    y_parts[y] = early[pl.ds(y * quarter, quarter)]

    arrived(4, rows(far, 0))
    sent.append(send(11, rows(far, 0), other))
    arrived(5, rows(far, 1))
    sent.append(send(12, rows(far, 1), other))
    arrived(11, rows(far_o, 0))
    arrived(12, rows(far_o, 1))
    forward(far_x, late, 0)

    three = y_parts.at[pl.ds(0, ny - 1)]
    pltpu.make_async_copy(three, three, sum_recv.at[0]).wait()
    firsts = jnp.sum(y_parts[...], axis=0)
    rest = jnp.zeros((z_parts.shape[1] - quarter - rows_p, LANES), jnp.float32)
    mine = [firsts[row] for row in range(quarter)] + [late[p] for p in range(rows_p)] + [rest]
    z_parts[z] = jnp.concatenate(mine, axis=0).astype(jnp.bfloat16)
    learn(levels - 1)

    def across(step):
        pltpu.make_async_remote_copy(
            src_ref=z_parts.at[z], dst_ref=z_parts.at[z], send_sem=sum_send.at[1], recv_sem=sum_recv.at[1],
            device_id=z_peer(step), device_id_type=MESH,
        ).start()

    def both_ways(step, carry):
        across(nz // 2 - step)
        across(step - nz // 2)
        return carry

    across(nz // 2)
    lax.fori_loop(1, nz // 2, both_ways, 0)
    for number, strip in enumerate(strips[:3]):
        backward(strip, early, number * rows_p)
    backward(far_x, late, 0)
    res_copy = pltpu.make_async_copy(mom, res_out, out_sem.at[2])
    res_copy.start()
    many = z_parts.at[pl.ds(0, nz - 1)]
    pltpu.make_async_copy(many, many, sum_recv.at[1]).wait()
    y_sums[y] = jnp.sum(z_parts[...].astype(jnp.float32), axis=0)

    def late_y(step, carry):
        pltpu.make_async_remote_copy(
            src_ref=y_sums.at[y], dst_ref=y_sums.at[y], send_sem=sum_send.at[2], recv_sem=sum_recv.at[2],
            device_id=y_peer(step), device_id_type=MESH,
        ).start()
        return carry

    lax.fori_loop(1, ny, late_y, 0)
    some = y_sums.at[pl.ds(0, ny - 1)]
    pltpu.make_async_copy(some, some, sum_recv.at[2]).wait()
    for number, strip in enumerate(strips[:3]):
        for p in range(rows_p):
            row = number * rows_p + p
            at_row = row % quarter
            total[strip * rows_p + p] = y_sums[row // quarter, at_row : at_row + 1]
    last = jnp.sum(y_sums[...], axis=0)
    for p in range(rows_p):
        total[far_x * rows_p + p] = last[quarter + p : quarter + p + 1]
    total_copy = pltpu.make_async_copy(total, total_out, out_sem.at[3])
    total_copy.start()

    for copy in sent:
        copy.wait_send()
    pltpu.make_async_copy(three, three, sum_send.at[0]).wait()
    pltpu.make_async_copy(many, many, sum_send.at[1]).wait()
    pltpu.make_async_copy(some, some, sum_send.at[2]).wait()
    for copy in bases_out:
        copy.wait()
    res_copy.wait()
    total_copy.wait()


def second_kernel(
    total, at, w, res_in, weight, target,
    update_hbm, res_hbm, blended_hbm,
    update, blended, out_sem,
):
    res_copy = pltpu.make_async_copy(res_in, res_hbm, out_sem.at[0])
    res_copy.start()
    rows_p, strips = w.shape[:2]
    outs = []
    for p in range(rows_p):
        at_rows = slice(p * BLOCK, (p + 1) * BLOCK)
        for g in range(strips):
            at_lanes = slice(g * LANES, (g + 1) * LANES)
            field = decode(total[g * rows_p + p], at[p, :, at_lanes], w[p, g])
            update[at_rows, at_lanes] = field
            moved = weight[at_rows, at_lanes].astype(jnp.float32) - update_rate * field
            mixed = (1.0 - polyak_rate) * target[at_rows, at_lanes].astype(jnp.float32) + polyak_rate * moved
            blended[at_rows, at_lanes] = mixed.astype(jnp.bfloat16)
        outs.append(pltpu.make_async_copy(update.at[at_rows], update_hbm.at[at_rows], out_sem.at[1 + 2 * p]))
        outs.append(pltpu.make_async_copy(blended.at[at_rows], blended_hbm.at[at_rows], out_sem.at[2 + 2 * p]))
        outs[-2].start()
        outs[-1].start()
    for copy in outs:
        copy.wait()
    res_copy.wait()


def shards(ny, nz, tokens, key_grad, momentum, key_weight, target, positions):
    anywhere = pl.BlockSpec(memory_space=pl.ANY)
    table = jnp.asarray(split_table())
    depth, feats = tokens.shape
    _, _, width = momentum.shape
    rows_p, col_blocks, keep = positions.shape
    strips = width // LANES
    rows = rows_p * strips
    at_shape, w_shape = (rows_p, BLOCK, width), (rows_p, strips, 2 * BLOCK, 2 * LANES)
    early = (strips - 1) * rows_p
    quarter = early // ny
    residual, total, at, w = pl.pallas_call(
        functools.partial(first_kernel, ny, nz),
        out_shape=(
            pltpu.VMEM((feats, width), jnp.float32),
            pltpu.VMEM((rows, 1, LANES), jnp.float32),
            pltpu.VMEM(at_shape, jnp.float32),
            pltpu.VMEM(w_shape, jnp.bfloat16),
        ),
        in_specs=[anywhere] * 5,
        out_specs=(anywhere,) * 4,
        scratch_shapes=[
            pltpu.VMEM((depth, feats), jnp.bfloat16),
            pltpu.VMEM((feats, depth), jnp.bfloat16),
            pltpu.VMEM((width, depth), jnp.bfloat16),
            pltpu.VMEM((feats, width), jnp.float32),
            pltpu.VMEM(at_shape, jnp.float32),
            pltpu.VMEM(w_shape, jnp.bfloat16),
            pltpu.VMEM((rows_p, col_blocks, keep), jnp.int32),
            pltpu.VMEM(table.shape, jnp.bfloat16),
            pltpu.VMEM((early, 1, LANES), jnp.float32),
            pltpu.VMEM((rows_p, 1, LANES), jnp.float32),
            pltpu.VMEM((ny, quarter, 1, LANES), jnp.float32),
            pltpu.VMEM((nz, 16, LANES), jnp.bfloat16),
            pltpu.VMEM((ny, 16, LANES), jnp.float32),
            pltpu.VMEM((rows, 1, LANES), jnp.float32),
            pltpu.SemaphoreType.DMA((5,)),
            pltpu.SemaphoreType.DMA((13,)),
            pltpu.SemaphoreType.DMA((13,)),
            pltpu.SemaphoreType.DMA((3,)),
            pltpu.SemaphoreType.DMA((3,)),
            pltpu.SemaphoreType.DMA((4,)),
            pltpu.SemaphoreType.REGULAR(((nz // 2).bit_length() - 2,)),
            pltpu.SemaphoreType.REGULAR(((nz // 2).bit_length() - 2,)),
        ],
        compiler_params=pltpu.CompilerParams(
            collective_id=0, has_side_effects=True, vmem_limit_bytes=54 * 1024 * 1024
        ),
        cost_estimate=pl.CostEstimate(flops=1_000_000_000, bytes_accessed=8_000_000, transcendentals=0),
        name="gather_encode_sum",
    )(tokens, key_grad.T, momentum[0], positions, table)
    in_vmem = pl.BlockSpec(memory_space=pltpu.VMEM)
    update, residual, blended = pl.pallas_call(
        second_kernel,
        out_shape=(
            jax.ShapeDtypeStruct((feats, width), jnp.float32),
            jax.ShapeDtypeStruct((feats, width), jnp.float32),
            jax.ShapeDtypeStruct((feats, width), jnp.bfloat16),
        ),
        in_specs=[in_vmem] * 3 + [anywhere] + [in_vmem] * 2,
        out_specs=(anywhere,) * 3,
        scratch_shapes=[
            pltpu.VMEM((feats, width), jnp.float32),
            pltpu.VMEM((feats, width), jnp.bfloat16),
            pltpu.SemaphoreType.DMA((1 + 2 * rows_p,)),
        ],
        compiler_params=pltpu.CompilerParams(vmem_limit_bytes=32 * 1024 * 1024),
        cost_estimate=pl.CostEstimate(flops=300_000_000, bytes_accessed=8_000_000, transcendentals=0),
        name="decode_blend",
    )(total, at, w, residual, key_weight, target)
    return (update, residual[None], blended)


def solution(mesh):
    in_specs = (
        P("rep", "tp"),
        P("rep", "tp"),
        P("rep", "tp", None),
        P("tp", None),
        P("tp", None),
        P("tp", None, None),
    )
    out_specs = (P("tp", None), P("rep", "tp", None), P("tp", None))
    body = functools.partial(shards, NY, mesh.shape["rep"] // NY)
    return jax.shard_map(body, mesh=mesh, in_specs=in_specs, out_specs=out_specs, check_vma=False)
```

```python
import functools

import jax
import jax.numpy as jnp
import ml_dtypes
import numpy as np
from jax import lax
from jax.experimental import pallas as pl
from jax.experimental.pallas import tpu as pltpu
from jax.sharding import PartitionSpec as P

BLOCK = 64
LANES = 128
NX, NY = 4, 4

momentum_decay = 0.9
polyak_rate = 0.25
update_rate = 0.1

MESH = pl.DeviceIdType.MESH
NT = (((1,), (1,)), ((), ()))


def split_table():
    index = np.arange(BLOCK, dtype=np.float64)
    angle = np.pi * (2.0 * index[:, None] + 1.0) * index[None, :] / (2.0 * BLOCK)
    scale = np.where(index == 0, np.sqrt(1.0 / BLOCK), np.sqrt(2.0 / BLOCK))
    table = np.cos(angle) * scale[None, :]
    high = table.astype(ml_dtypes.bfloat16)
    low = (table - high.astype(np.float64)).astype(ml_dtypes.bfloat16)
    return np.concatenate([high, low], axis=0)


def split_rows(value):
    high = value.astype(jnp.bfloat16)
    low = (value - high.astype(jnp.float32)).astype(jnp.bfloat16)
    return high, low


def strip_of(strip):
    return pl.ds(pl.multiple_of(strip * LANES, LANES), LANES)


def make_bases(pos_ref, table_ref, at_ref, w_ref):
    row_blocks, col_blocks, keep = pos_ref.shape
    width = col_blocks * keep
    lane = lax.broadcasted_iota(jnp.int32, (BLOCK, LANES), 1)
    level = lax.broadcasted_iota(jnp.int32, (BLOCK, width), 0)
    table = table_ref[...]
    flat = jnp.concatenate([pos_ref[:, b, :] for b in range(col_blocks)], axis=1)
    for p in range(row_blocks):
        row = flat[p : p + 1, :]
        first = jnp.where(level == (row >> 6), 1.0, 0.0).astype(jnp.bfloat16)
        second = jnp.where(level == (row & 63), 1.0, 0.0).astype(jnp.bfloat16)
        picked = jnp.dot(table, first, preferred_element_type=jnp.float32)
        at_ref[p] = picked[:BLOCK] + picked[BLOCK:]
        other = jnp.dot(table, second, preferred_element_type=jnp.float32)
        for g in range(width // LANES):
            for part in range(2):
                piece = other[part * BLOCK : (part + 1) * BLOCK, g * LANES : (g + 1) * LANES]
                top = jnp.where(lane < BLOCK, piece, 0.0).astype(jnp.bfloat16)
                low = jnp.where(lane < BLOCK, 0.0, piece).astype(jnp.bfloat16)
                w_ref[p, g, 0:BLOCK, part * LANES : (part + 1) * LANES] = top
                w_ref[p, g, BLOCK : 2 * BLOCK, part * LANES : (part + 1) * LANES] = low


def encode(block, at, w):
    high, low = split_rows(block)
    both = jnp.dot(jnp.concatenate([high, low], axis=0), w, preferred_element_type=jnp.float32)
    mixed = both[:BLOCK, :LANES] + both[:BLOCK, LANES:] + both[BLOCK:, :LANES]
    return jnp.sum(mixed * at, axis=0, keepdims=True)


def decode(values, at, w):
    high, low = split_rows(at * values)
    rows = jnp.concatenate(
        [jnp.concatenate([high, high], axis=1), jnp.concatenate([low, jnp.zeros_like(low)], axis=1)], axis=0
    )
    both = lax.dot_general(rows, w, NT, preferred_element_type=jnp.float32)
    return both[:BLOCK] + both[BLOCK:]


def first_kernel(
    ny, nz,
    tok_hbm, grad_hbm, mom_hbm, pos_hbm, table_hbm,
    res_out, total_out, at_out, w_out,
    tok, tok_t, gall, mom, at, w, pos, table, early, late, y_parts, y_lasts, z_parts, y_sums, total,
    load_sem, send_sem, recv_sem, sum_send, sum_recv, out_sem, know_down, know_up,
):
    rep, tp = lax.axis_index("rep"), lax.axis_index("tp")
    z, y = rep // ny, lax.rem(rep, ny)
    x, core = tp // 2, lax.rem(tp, 2)
    right = lax.rem(x + 1, NX) * 2 + core
    left = lax.rem(x + NX - 1, NX) * 2 + core
    far = lax.rem(x + 2, NX) * 2 + core
    other = 2 * x + 1 - core
    rows_p = at.shape[0]
    quarter, share = early.shape[0] // ny, rows_p // ny

    def z_peer(step):
        step = step % nz if isinstance(step, int) else step
        return {"rep": lax.rem(z + step + nz, nz) * ny + y}

    def y_peer(step):
        return {"rep": z * ny + lax.rem(y + step + ny, ny)}

    def tell(semaphore, device):
        pl.semaphore_signal(semaphore, inc=1, device_id=device, device_id_type=MESH)

    own_rows = gall.at[pl.ds(pl.multiple_of(tp * BLOCK, BLOCK), BLOCK)]
    loads = [
        pltpu.make_async_copy(pos_hbm, pos, load_sem.at[0]),
        pltpu.make_async_copy(table_hbm, table, load_sem.at[1]),
        pltpu.make_async_copy(grad_hbm, own_rows, load_sem.at[2]),
        pltpu.make_async_copy(tok_hbm, tok, load_sem.at[3]),
        pltpu.make_async_copy(mom_hbm, mom, load_sem.at[4]),
    ]

    loads[2].start()
    barrier = pltpu.get_barrier_semaphore()
    for peer in (right, left, other):
        tell(barrier, {"tp": peer})
    for step in (2, -2, 1, -1):
        tell(barrier, z_peer(step))
    for step in range(1, ny):
        tell(barrier, y_peer(step))
    for number in (3, 4, 0, 1):
        loads[number].start()

    loads[2].wait()
    pl.semaphore_wait(barrier, 3 + 4 + ny - 1)

    levels = know_down.shape[0]

    def pass_on(level):
        tell(know_down.at[level], z_peer(2 << level))
        tell(know_up.at[level], z_peer(-(2 << level)))

    def learn(level):
        pl.semaphore_wait(know_down.at[level], 1)
        pl.semaphore_wait(know_up.at[level], 1)
        if level + 1 < levels:
            pass_on(level + 1)

    pass_on(0)
    half = BLOCK // 2

    def rows(owner, part_at):
        return gall.at[pl.ds(pl.multiple_of(owner * BLOCK + part_at * half, half), half)]

    def send(number, block, device):
        copy = pltpu.make_async_remote_copy(
            src_ref=block, dst_ref=block, send_sem=send_sem.at[number], recv_sem=recv_sem.at[number],
            device_id={"tp": device}, device_id_type=MESH,
        )
        copy.start()
        return copy

    def arrived(number, block):
        pltpu.make_async_remote_copy(
            src_ref=block, dst_ref=block, send_sem=send_sem.at[number], recv_sem=recv_sem.at[number],
            device_id={"tp": other}, device_id_type=MESH,
        ).wait_recv()

    sent = [
        send(0, rows(tp, 0), right),
        send(2, rows(tp, 1), left),
        send(1, rows(tp, 1), right),
        send(3, rows(tp, 0), left),
        send(6, own_rows, other),
    ]

    loads[3].wait()
    depth = tok.shape[0]
    for at_row in range(0, depth, 256):
        tok_t[:, at_row : at_row + 256] = tok[at_row : at_row + 256, :].T
    loads[4].wait()
    loads[0].wait()
    loads[1].wait()
    make_bases(pos, table, at, w)
    bases_out = [
        pltpu.make_async_copy(at, at_out, out_sem.at[0]),
        pltpu.make_async_copy(w, w_out, out_sem.at[1]),
    ]
    for copy in bases_out:
        copy.start()
    learn(0)

    arrived(0, rows(left, 0))
    sent.append(send(4, rows(left, 0), right))
    arrived(2, rows(right, 1))
    sent.append(send(5, rows(right, 1), left))
    sent.append(send(7, rows(left, 0), other))
    sent.append(send(10, rows(right, 1), other))
    arrived(1, rows(left, 1))
    sent.append(send(8, rows(left, 1), other))
    arrived(3, rows(right, 0))
    sent.append(send(9, rows(right, 0), other))

    def forward(strip, keep, base):
        grads = gall[pl.ds(pl.multiple_of(strip * LANES, LANES), LANES), :]
        gradient = lax.dot_general(tok_t[...], grads, NT, preferred_element_type=jnp.float32)
        moment = momentum_decay * mom[:, strip_of(strip)] + gradient
        mom[:, strip_of(strip)] = moment
        for p in range(rows_p):
            block = moment[p * BLOCK : (p + 1) * BLOCK]
            keep[base + p] = encode(block, at[p, :, strip_of(strip)], w[p, strip])

    def backward(strip, keep, base):
        for p in range(rows_p):
            field = decode(keep[base + p], at[p, :, strip_of(strip)], w[p, strip])
            mom[p * BLOCK : (p + 1) * BLOCK, strip_of(strip)] = (
                mom[p * BLOCK : (p + 1) * BLOCK, strip_of(strip)] - field
            )

    left_x, right_x, far_x = lax.rem(x + NX - 1, NX), lax.rem(x + 1, NX), lax.rem(x + 2, NX)
    left_o, right_o, far_o = left_x * 2 + 1 - core, right_x * 2 + 1 - core, far_x * 2 + 1 - core
    strips = (x, left_x, right_x, far_x)

    arrived(6, gall.at[pl.ds(pl.multiple_of(other * BLOCK, BLOCK), BLOCK)])
    forward(x, early, 0)
    for level in range(1, levels - 1):
        learn(level)
    arrived(7, rows(left_o, 0))
    arrived(8, rows(left_o, 1))
    forward(left_x, early, rows_p)
    arrived(9, rows(right_o, 0))
    arrived(10, rows(right_o, 1))
    forward(right_x, early, 2 * rows_p)

    def early_y(step, carry):
        peer = lax.rem(y + step, ny)
        pltpu.make_async_remote_copy(
            src_ref=early.at[pl.ds(peer * quarter, quarter)], dst_ref=y_parts.at[y],
            send_sem=sum_send.at[0], recv_sem=sum_recv.at[0], device_id=y_peer(step), device_id_type=MESH,
        ).start()
        return carry

    lax.fori_loop(1, ny, early_y, 0)
    y_parts[y] = early[pl.ds(y * quarter, quarter)]

    arrived(4, rows(far, 0))
    sent.append(send(11, rows(far, 0), other))
    arrived(5, rows(far, 1))
    sent.append(send(12, rows(far, 1), other))
    arrived(11, rows(far_o, 0))
    arrived(12, rows(far_o, 1))
    forward(far_x, late, 0)

    def last_y(step, carry):
        peer = lax.rem(y + step, ny)
        pltpu.make_async_remote_copy(
            src_ref=late.at[pl.ds(peer * share, share)], dst_ref=y_lasts.at[y],
            send_sem=sum_send.at[3], recv_sem=sum_recv.at[3], device_id=y_peer(step), device_id_type=MESH,
        ).start()
        return carry

    lax.fori_loop(1, ny, last_y, 0)
    y_lasts[y] = late[pl.ds(y * share, share)]
    for number, strip in enumerate(strips[:3]):
        backward(strip, early, number * rows_p)

    three = y_parts.at[pl.ds(0, ny - 1)]
    pltpu.make_async_copy(three, three, sum_recv.at[0]).wait()
    firsts = jnp.sum(y_parts[...], axis=0)
    others = y_lasts.at[pl.ds(0, ny - 1)]
    pltpu.make_async_copy(others, others, sum_recv.at[3]).wait()
    lasts = jnp.sum(y_lasts[...], axis=0)
    mine = [firsts[row] for row in range(quarter)] + [lasts[row] for row in range(share)]
    z_parts[z] = jnp.concatenate(mine, axis=0).astype(jnp.bfloat16)
    learn(levels - 1)

    def across(step):
        pltpu.make_async_remote_copy(
            src_ref=z_parts.at[z], dst_ref=z_parts.at[z], send_sem=sum_send.at[1], recv_sem=sum_recv.at[1],
            device_id=z_peer(step), device_id_type=MESH,
        ).start()

    def both_ways(step, carry):
        across(nz // 2 - step)
        across(step - nz // 2)
        return carry

    across(nz // 2)
    lax.fori_loop(1, nz // 2, both_ways, 0)
    backward(far_x, late, 0)
    res_copy = pltpu.make_async_copy(mom, res_out, out_sem.at[2])
    res_copy.start()
    many = z_parts.at[pl.ds(0, nz - 1)]
    pltpu.make_async_copy(many, many, sum_recv.at[1]).wait()
    y_sums[y] = jnp.sum(z_parts[...].astype(jnp.float32), axis=0)

    def late_y(step, carry):
        pltpu.make_async_remote_copy(
            src_ref=y_sums.at[y], dst_ref=y_sums.at[y], send_sem=sum_send.at[2], recv_sem=sum_recv.at[2],
            device_id=y_peer(step), device_id_type=MESH,
        ).start()
        return carry

    lax.fori_loop(1, ny, late_y, 0)
    some = y_sums.at[pl.ds(0, ny - 1)]
    pltpu.make_async_copy(some, some, sum_recv.at[2]).wait()
    for number, strip in enumerate(strips[:3]):
        for p in range(rows_p):
            row = number * rows_p + p
            at_row = row % quarter
            total[strip * rows_p + p] = y_sums[row // quarter, at_row : at_row + 1]
    for p in range(rows_p):
        at_row = quarter + p % share
        total[far_x * rows_p + p] = y_sums[p // share, at_row : at_row + 1]
    total_copy = pltpu.make_async_copy(total, total_out, out_sem.at[3])
    total_copy.start()

    for copy in sent:
        copy.wait_send()
    pltpu.make_async_copy(three, three, sum_send.at[0]).wait()
    pltpu.make_async_copy(others, others, sum_send.at[3]).wait()
    pltpu.make_async_copy(many, many, sum_send.at[1]).wait()
    pltpu.make_async_copy(some, some, sum_send.at[2]).wait()
    for copy in bases_out:
        copy.wait()
    res_copy.wait()
    total_copy.wait()


def second_kernel(
    total, at, w, res_in, weight, target,
    update_hbm, res_hbm, blended_hbm,
    update, blended, out_sem,
):
    res_copy = pltpu.make_async_copy(res_in, res_hbm, out_sem.at[0])
    res_copy.start()
    rows_p, strips = w.shape[:2]
    outs = []
    for p in range(rows_p):
        at_rows = slice(p * BLOCK, (p + 1) * BLOCK)
        for g in range(strips):
            at_lanes = slice(g * LANES, (g + 1) * LANES)
            field = decode(total[g * rows_p + p], at[p, :, at_lanes], w[p, g])
            update[at_rows, at_lanes] = field
            moved = weight[at_rows, at_lanes].astype(jnp.float32) - update_rate * field
            mixed = (1.0 - polyak_rate) * target[at_rows, at_lanes].astype(jnp.float32) + polyak_rate * moved
            blended[at_rows, at_lanes] = mixed.astype(jnp.bfloat16)
        outs.append(pltpu.make_async_copy(update.at[at_rows], update_hbm.at[at_rows], out_sem.at[1 + 2 * p]))
        outs.append(pltpu.make_async_copy(blended.at[at_rows], blended_hbm.at[at_rows], out_sem.at[2 + 2 * p]))
        outs[-2].start()
        outs[-1].start()
    for copy in outs:
        copy.wait()
    res_copy.wait()


def shards(ny, nz, tokens, key_grad, momentum, key_weight, target, positions):
    anywhere = pl.BlockSpec(memory_space=pl.ANY)
    table = jnp.asarray(split_table())
    depth, feats = tokens.shape
    _, _, width = momentum.shape
    rows_p, col_blocks, keep = positions.shape
    strips = width // LANES
    rows = rows_p * strips
    at_shape, w_shape = (rows_p, BLOCK, width), (rows_p, strips, 2 * BLOCK, 2 * LANES)
    early = (strips - 1) * rows_p
    quarter = early // ny
    residual, total, at, w = pl.pallas_call(
        functools.partial(first_kernel, ny, nz),
        out_shape=(
            pltpu.VMEM((feats, width), jnp.float32),
            pltpu.VMEM((rows, 1, LANES), jnp.float32),
            pltpu.VMEM(at_shape, jnp.float32),
            pltpu.VMEM(w_shape, jnp.bfloat16),
        ),
        in_specs=[anywhere] * 5,
        out_specs=(anywhere,) * 4,
        scratch_shapes=[
            pltpu.VMEM((depth, feats), jnp.bfloat16),
            pltpu.VMEM((feats, depth), jnp.bfloat16),
            pltpu.VMEM((width, depth), jnp.bfloat16),
            pltpu.VMEM((feats, width), jnp.float32),
            pltpu.VMEM(at_shape, jnp.float32),
            pltpu.VMEM(w_shape, jnp.bfloat16),
            pltpu.VMEM((rows_p, col_blocks, keep), jnp.int32),
            pltpu.VMEM(table.shape, jnp.bfloat16),
            pltpu.VMEM((early, 1, LANES), jnp.float32),
            pltpu.VMEM((rows_p, 1, LANES), jnp.float32),
            pltpu.VMEM((ny, quarter, 1, LANES), jnp.float32),
            pltpu.VMEM((ny, rows_p // ny, 1, LANES), jnp.float32),
            pltpu.VMEM((nz, rows // ny, LANES), jnp.bfloat16),
            pltpu.VMEM((ny, rows // ny, LANES), jnp.float32),
            pltpu.VMEM((rows, 1, LANES), jnp.float32),
            pltpu.SemaphoreType.DMA((5,)),
            pltpu.SemaphoreType.DMA((13,)),
            pltpu.SemaphoreType.DMA((13,)),
            pltpu.SemaphoreType.DMA((4,)),
            pltpu.SemaphoreType.DMA((4,)),
            pltpu.SemaphoreType.DMA((4,)),
            pltpu.SemaphoreType.REGULAR(((nz // 2).bit_length() - 2,)),
            pltpu.SemaphoreType.REGULAR(((nz // 2).bit_length() - 2,)),
        ],
        compiler_params=pltpu.CompilerParams(
            collective_id=0, has_side_effects=True, vmem_limit_bytes=54 * 1024 * 1024
        ),
        cost_estimate=pl.CostEstimate(flops=1_000_000_000, bytes_accessed=8_000_000, transcendentals=0),
        name="gather_encode_sum",
    )(tokens, key_grad.T, momentum[0], positions, table)
    in_vmem = pl.BlockSpec(memory_space=pltpu.VMEM)
    update, residual, blended = pl.pallas_call(
        second_kernel,
        out_shape=(
            jax.ShapeDtypeStruct((feats, width), jnp.float32),
            jax.ShapeDtypeStruct((feats, width), jnp.float32),
            jax.ShapeDtypeStruct((feats, width), jnp.bfloat16),
        ),
        in_specs=[in_vmem] * 3 + [anywhere] + [in_vmem] * 2,
        out_specs=(anywhere,) * 3,
        scratch_shapes=[
            pltpu.VMEM((feats, width), jnp.float32),
            pltpu.VMEM((feats, width), jnp.bfloat16),
            pltpu.SemaphoreType.DMA((1 + 2 * rows_p,)),
        ],
        compiler_params=pltpu.CompilerParams(vmem_limit_bytes=32 * 1024 * 1024),
        cost_estimate=pl.CostEstimate(flops=300_000_000, bytes_accessed=8_000_000, transcendentals=0),
        name="decode_blend",
    )(total, at, w, residual, key_weight, target)
    return (update, residual[None], blended)


def solution(mesh):
    in_specs = (
        P("rep", "tp"),
        P("rep", "tp"),
        P("rep", "tp", None),
        P("tp", None),
        P("tp", None),
        P("tp", None, None),
    )
    out_specs = (P("tp", None), P("rep", "tp", None), P("tp", None))
    body = functools.partial(shards, NY, mesh.shape["rep"] // NY)
    return jax.shard_map(body, mesh=mesh, in_specs=in_specs, out_specs=out_specs, check_vma=False)
```

```python
import functools

import jax
import jax.numpy as jnp
import ml_dtypes
import numpy as np
from jax import lax
from jax.experimental import pallas as pl
from jax.experimental.pallas import tpu as pltpu
from jax.sharding import PartitionSpec as P

BLOCK = 64
LANES = 128
NX, NY = 4, 4

momentum_decay = 0.9
polyak_rate = 0.25
update_rate = 0.1

MESH = pl.DeviceIdType.MESH
NT = (((1,), (1,)), ((), ()))


def split_table():
    index = np.arange(BLOCK, dtype=np.float64)
    angle = np.pi * (2.0 * index[:, None] + 1.0) * index[None, :] / (2.0 * BLOCK)
    scale = np.where(index == 0, np.sqrt(1.0 / BLOCK), np.sqrt(2.0 / BLOCK))
    table = np.cos(angle) * scale[None, :]
    high = table.astype(ml_dtypes.bfloat16)
    low = (table - high.astype(np.float64)).astype(ml_dtypes.bfloat16)
    return np.concatenate([high, low], axis=0)


def split_rows(value):
    high = value.astype(jnp.bfloat16)
    low = (value - high.astype(jnp.float32)).astype(jnp.bfloat16)
    return high, low


def strip_of(strip):
    return pl.ds(pl.multiple_of(strip * LANES, LANES), LANES)


def make_bases(pos_ref, table_ref, at_ref, w_ref):
    row_blocks, col_blocks, keep = pos_ref.shape
    width = col_blocks * keep
    lane = lax.broadcasted_iota(jnp.int32, (BLOCK, LANES), 1)
    level = lax.broadcasted_iota(jnp.int32, (BLOCK, width), 0)
    table = table_ref[...]
    flat = jnp.concatenate([pos_ref[:, b, :] for b in range(col_blocks)], axis=1)
    for p in range(row_blocks):
        row = flat[p : p + 1, :]
        first = jnp.where(level == (row >> 6), 1.0, 0.0).astype(jnp.bfloat16)
        second = jnp.where(level == (row & 63), 1.0, 0.0).astype(jnp.bfloat16)
        picked = jnp.dot(table, first, preferred_element_type=jnp.float32)
        at_ref[p] = picked[:BLOCK] + picked[BLOCK:]
        other = jnp.dot(table, second, preferred_element_type=jnp.float32)
        for g in range(width // LANES):
            for part in range(2):
                piece = other[part * BLOCK : (part + 1) * BLOCK, g * LANES : (g + 1) * LANES]
                top = jnp.where(lane < BLOCK, piece, 0.0).astype(jnp.bfloat16)
                low = jnp.where(lane < BLOCK, 0.0, piece).astype(jnp.bfloat16)
                w_ref[p, g, 0:BLOCK, part * LANES : (part + 1) * LANES] = top
                w_ref[p, g, BLOCK : 2 * BLOCK, part * LANES : (part + 1) * LANES] = low


def encode(block, at, w):
    high, low = split_rows(block)
    both = jnp.dot(jnp.concatenate([high, low], axis=0), w, preferred_element_type=jnp.float32)
    mixed = both[:BLOCK, :LANES] + both[:BLOCK, LANES:] + both[BLOCK:, :LANES]
    return jnp.sum(mixed * at, axis=0, keepdims=True)


def decode(values, at, w):
    high, low = split_rows(at * values)
    rows = jnp.concatenate(
        [jnp.concatenate([high, high], axis=1), jnp.concatenate([low, jnp.zeros_like(low)], axis=1)], axis=0
    )
    both = lax.dot_general(rows, w, NT, preferred_element_type=jnp.float32)
    return both[:BLOCK] + both[BLOCK:]


def first_kernel(
    ny, nz,
    tok_hbm, grad_hbm, mom_hbm, pos_hbm, table_hbm,
    res_out, total_out, at_out, w_out,
    tok, tok_t, gall, mom, at, w, pos, table, early, late, y_parts, y_lasts, z_parts, y_sums, total,
    load_sem, send_sem, recv_sem, sum_send, sum_recv, out_sem, know_y, know_down, know_up,
):
    rep, tp = lax.axis_index("rep"), lax.axis_index("tp")
    z, y = rep // ny, lax.rem(rep, ny)
    x, core = tp // 2, lax.rem(tp, 2)
    right = lax.rem(x + 1, NX) * 2 + core
    left = lax.rem(x + NX - 1, NX) * 2 + core
    far = lax.rem(x + 2, NX) * 2 + core
    other = 2 * x + 1 - core
    rows_p = at.shape[0]
    quarter, share = early.shape[0] // ny, rows_p // ny

    def z_peer(step):
        step = step % nz if isinstance(step, int) else step
        return {"rep": lax.rem(z + step + nz, nz) * ny + y}

    def y_peer(step):
        return {"rep": z * ny + lax.rem(y + step + ny, ny)}

    def tell(semaphore, device):
        pl.semaphore_signal(semaphore, inc=1, device_id=device, device_id_type=MESH)

    own_rows = gall.at[pl.ds(pl.multiple_of(tp * BLOCK, BLOCK), BLOCK)]
    loads = [
        pltpu.make_async_copy(pos_hbm, pos, load_sem.at[0]),
        pltpu.make_async_copy(table_hbm, table, load_sem.at[1]),
        pltpu.make_async_copy(grad_hbm, own_rows, load_sem.at[2]),
        pltpu.make_async_copy(tok_hbm, tok, load_sem.at[3]),
        pltpu.make_async_copy(mom_hbm, mom, load_sem.at[4]),
    ]

    loads[2].start()
    barrier = pltpu.get_barrier_semaphore()
    for peer in (right, left, other):
        tell(barrier, {"tp": peer})
    for step in (1, -1):
        tell(barrier, z_peer(step))
        tell(barrier, y_peer(step))
    for number in (3, 4, 0, 1):
        loads[number].start()

    loads[2].wait()
    pl.semaphore_wait(barrier, 7)

    levels = know_down.shape[0]

    def pass_on(level):
        tell(know_down.at[level], z_peer(1 << level))
        tell(know_up.at[level], z_peer(-(1 << level)))

    def learn(level):
        pl.semaphore_wait(know_down.at[level], 1)
        pl.semaphore_wait(know_up.at[level], 1)
        if level + 1 < levels:
            pass_on(level + 1)

    tell(know_y, y_peer(-1))
    pass_on(0)
    half = BLOCK // 2

    def rows(owner, part_at):
        return gall.at[pl.ds(pl.multiple_of(owner * BLOCK + part_at * half, half), half)]

    def send(number, block, device):
        copy = pltpu.make_async_remote_copy(
            src_ref=block, dst_ref=block, send_sem=send_sem.at[number], recv_sem=recv_sem.at[number],
            device_id={"tp": device}, device_id_type=MESH,
        )
        copy.start()
        return copy

    def arrived(number, block):
        pltpu.make_async_remote_copy(
            src_ref=block, dst_ref=block, send_sem=send_sem.at[number], recv_sem=recv_sem.at[number],
            device_id={"tp": other}, device_id_type=MESH,
        ).wait_recv()

    sent = [
        send(0, rows(tp, 0), right),
        send(2, rows(tp, 1), left),
        send(1, rows(tp, 1), right),
        send(3, rows(tp, 0), left),
        send(6, own_rows, other),
    ]

    loads[3].wait()
    depth = tok.shape[0]
    for at_row in range(0, depth, 256):
        tok_t[:, at_row : at_row + 256] = tok[at_row : at_row + 256, :].T
    loads[4].wait()
    pl.semaphore_wait(know_y, 1)
    learn(0)
    loads[0].wait()
    loads[1].wait()
    make_bases(pos, table, at, w)
    bases_out = [
        pltpu.make_async_copy(at, at_out, out_sem.at[0]),
        pltpu.make_async_copy(w, w_out, out_sem.at[1]),
    ]
    for copy in bases_out:
        copy.start()
    learn(1)

    arrived(0, rows(left, 0))
    sent.append(send(4, rows(left, 0), right))
    arrived(2, rows(right, 1))
    sent.append(send(5, rows(right, 1), left))
    sent.append(send(7, rows(left, 0), other))
    sent.append(send(10, rows(right, 1), other))
    arrived(1, rows(left, 1))
    sent.append(send(8, rows(left, 1), other))
    arrived(3, rows(right, 0))
    sent.append(send(9, rows(right, 0), other))

    def forward(strip, keep, base):
        grads = gall[pl.ds(pl.multiple_of(strip * LANES, LANES), LANES), :]
        gradient = lax.dot_general(tok_t[...], grads, NT, preferred_element_type=jnp.float32)
        moment = momentum_decay * mom[:, strip_of(strip)] + gradient
        mom[:, strip_of(strip)] = moment
        for p in range(rows_p):
            block = moment[p * BLOCK : (p + 1) * BLOCK]
            keep[base + p] = encode(block, at[p, :, strip_of(strip)], w[p, strip])

    def backward(strip, keep, base):
        for p in range(rows_p):
            field = decode(keep[base + p], at[p, :, strip_of(strip)], w[p, strip])
            mom[p * BLOCK : (p + 1) * BLOCK, strip_of(strip)] = (
                mom[p * BLOCK : (p + 1) * BLOCK, strip_of(strip)] - field
            )

    left_x, right_x, far_x = lax.rem(x + NX - 1, NX), lax.rem(x + 1, NX), lax.rem(x + 2, NX)
    left_o, right_o, far_o = left_x * 2 + 1 - core, right_x * 2 + 1 - core, far_x * 2 + 1 - core
    strips = (x, left_x, right_x, far_x)

    arrived(6, gall.at[pl.ds(pl.multiple_of(other * BLOCK, BLOCK), BLOCK)])
    forward(x, early, 0)
    arrived(7, rows(left_o, 0))
    arrived(8, rows(left_o, 1))
    forward(left_x, early, rows_p)
    for level in range(2, levels - 1):
        learn(level)
    arrived(9, rows(right_o, 0))
    arrived(10, rows(right_o, 1))
    forward(right_x, early, 2 * rows_p)

    def early_y(step, carry):
        peer = lax.rem(y + step, ny)
        pltpu.make_async_remote_copy(
            src_ref=early.at[pl.ds(peer * quarter, quarter)], dst_ref=y_parts.at[y],
            send_sem=sum_send.at[0], recv_sem=sum_recv.at[0], device_id=y_peer(step), device_id_type=MESH,
        ).start()
        return carry

    lax.fori_loop(1, ny, early_y, 0)
    y_parts[y] = early[pl.ds(y * quarter, quarter)]

    arrived(4, rows(far, 0))
    sent.append(send(11, rows(far, 0), other))
    arrived(5, rows(far, 1))
    sent.append(send(12, rows(far, 1), other))
    arrived(11, rows(far_o, 0))
    arrived(12, rows(far_o, 1))
    forward(far_x, late, 0)

    def last_y(step, carry):
        peer = lax.rem(y + step, ny)
        pltpu.make_async_remote_copy(
            src_ref=late.at[pl.ds(peer * share, share)], dst_ref=y_lasts.at[y],
            send_sem=sum_send.at[3], recv_sem=sum_recv.at[3], device_id=y_peer(step), device_id_type=MESH,
        ).start()
        return carry

    lax.fori_loop(1, ny, last_y, 0)
    y_lasts[y] = late[pl.ds(y * share, share)]
    for number, strip in enumerate(strips[:3]):
        backward(strip, early, number * rows_p)

    three = y_parts.at[pl.ds(0, ny - 1)]
    pltpu.make_async_copy(three, three, sum_recv.at[0]).wait()
    firsts = jnp.sum(y_parts[...], axis=0)
    others = y_lasts.at[pl.ds(0, ny - 1)]
    pltpu.make_async_copy(others, others, sum_recv.at[3]).wait()
    lasts = jnp.sum(y_lasts[...], axis=0)
    mine = [firsts[row] for row in range(quarter)] + [lasts[row] for row in range(share)]
    z_parts[z] = jnp.concatenate(mine, axis=0).astype(jnp.bfloat16)
    learn(levels - 1)

    def across(step):
        pltpu.make_async_remote_copy(
            src_ref=z_parts.at[z], dst_ref=z_parts.at[z], send_sem=sum_send.at[1], recv_sem=sum_recv.at[1],
            device_id=z_peer(step), device_id_type=MESH,
        ).start()

    def both_ways(step, carry):
        across(nz // 2 - step)
        across(step - nz // 2)
        return carry

    across(nz // 2)
    lax.fori_loop(1, nz // 2, both_ways, 0)
    backward(far_x, late, 0)
    res_copy = pltpu.make_async_copy(mom, res_out, out_sem.at[2])
    res_copy.start()
    many = z_parts.at[pl.ds(0, nz - 1)]
    pltpu.make_async_copy(many, many, sum_recv.at[1]).wait()
    y_sums[y] = jnp.sum(z_parts[...].astype(jnp.float32), axis=0)

    def late_y(step, carry):
        pltpu.make_async_remote_copy(
            src_ref=y_sums.at[y], dst_ref=y_sums.at[y], send_sem=sum_send.at[2], recv_sem=sum_recv.at[2],
            device_id=y_peer(step), device_id_type=MESH,
        ).start()
        return carry

    lax.fori_loop(1, ny, late_y, 0)
    some = y_sums.at[pl.ds(0, ny - 1)]
    pltpu.make_async_copy(some, some, sum_recv.at[2]).wait()
    for number, strip in enumerate(strips[:3]):
        for p in range(rows_p):
            row = number * rows_p + p
            at_row = row % quarter
            total[strip * rows_p + p] = y_sums[row // quarter, at_row : at_row + 1]
    for p in range(rows_p):
        at_row = quarter + p % share
        total[far_x * rows_p + p] = y_sums[p // share, at_row : at_row + 1]
    total_copy = pltpu.make_async_copy(total, total_out, out_sem.at[3])
    total_copy.start()

    for copy in sent:
        copy.wait_send()
    pltpu.make_async_copy(three, three, sum_send.at[0]).wait()
    pltpu.make_async_copy(others, others, sum_send.at[3]).wait()
    pltpu.make_async_copy(many, many, sum_send.at[1]).wait()
    pltpu.make_async_copy(some, some, sum_send.at[2]).wait()
    for copy in bases_out:
        copy.wait()
    res_copy.wait()
    total_copy.wait()


def second_kernel(
    total, at, w, res_in, weight, target,
    update_hbm, res_hbm, blended_hbm,
    update, blended, out_sem,
):
    res_copy = pltpu.make_async_copy(res_in, res_hbm, out_sem.at[0])
    res_copy.start()
    rows_p, strips = w.shape[:2]
    outs = []
    for p in range(rows_p):
        at_rows = slice(p * BLOCK, (p + 1) * BLOCK)
        for g in range(strips):
            at_lanes = slice(g * LANES, (g + 1) * LANES)
            field = decode(total[g * rows_p + p], at[p, :, at_lanes], w[p, g])
            update[at_rows, at_lanes] = field
            moved = weight[at_rows, at_lanes].astype(jnp.float32) - update_rate * field
            mixed = (1.0 - polyak_rate) * target[at_rows, at_lanes].astype(jnp.float32) + polyak_rate * moved
            blended[at_rows, at_lanes] = mixed.astype(jnp.bfloat16)
        outs.append(pltpu.make_async_copy(update.at[at_rows], update_hbm.at[at_rows], out_sem.at[1 + 2 * p]))
        outs.append(pltpu.make_async_copy(blended.at[at_rows], blended_hbm.at[at_rows], out_sem.at[2 + 2 * p]))
        outs[-2].start()
        outs[-1].start()
    for copy in outs:
        copy.wait()
    res_copy.wait()


def shards(ny, nz, tokens, key_grad, momentum, key_weight, target, positions):
    anywhere = pl.BlockSpec(memory_space=pl.ANY)
    table = jnp.asarray(split_table())
    depth, feats = tokens.shape
    _, _, width = momentum.shape
    rows_p, col_blocks, keep = positions.shape
    strips = width // LANES
    rows = rows_p * strips
    at_shape, w_shape = (rows_p, BLOCK, width), (rows_p, strips, 2 * BLOCK, 2 * LANES)
    early = (strips - 1) * rows_p
    quarter = early // ny
    residual, total, at, w = pl.pallas_call(
        functools.partial(first_kernel, ny, nz),
        out_shape=(
            pltpu.VMEM((feats, width), jnp.float32),
            pltpu.VMEM((rows, 1, LANES), jnp.float32),
            pltpu.VMEM(at_shape, jnp.float32),
            pltpu.VMEM(w_shape, jnp.bfloat16),
        ),
        in_specs=[anywhere] * 5,
        out_specs=(anywhere,) * 4,
        scratch_shapes=[
            pltpu.VMEM((depth, feats), jnp.bfloat16),
            pltpu.VMEM((feats, depth), jnp.bfloat16),
            pltpu.VMEM((width, depth), jnp.bfloat16),
            pltpu.VMEM((feats, width), jnp.float32),
            pltpu.VMEM(at_shape, jnp.float32),
            pltpu.VMEM(w_shape, jnp.bfloat16),
            pltpu.VMEM((rows_p, col_blocks, keep), jnp.int32),
            pltpu.VMEM(table.shape, jnp.bfloat16),
            pltpu.VMEM((early, 1, LANES), jnp.float32),
            pltpu.VMEM((rows_p, 1, LANES), jnp.float32),
            pltpu.VMEM((ny, quarter, 1, LANES), jnp.float32),
            pltpu.VMEM((ny, rows_p // ny, 1, LANES), jnp.float32),
            pltpu.VMEM((nz, rows // ny, LANES), jnp.bfloat16),
            pltpu.VMEM((ny, rows // ny, LANES), jnp.float32),
            pltpu.VMEM((rows, 1, LANES), jnp.float32),
            pltpu.SemaphoreType.DMA((5,)),
            pltpu.SemaphoreType.DMA((13,)),
            pltpu.SemaphoreType.DMA((13,)),
            pltpu.SemaphoreType.DMA((4,)),
            pltpu.SemaphoreType.DMA((4,)),
            pltpu.SemaphoreType.DMA((4,)),
            pltpu.SemaphoreType.REGULAR,
            pltpu.SemaphoreType.REGULAR(((nz // 2).bit_length() - 1,)),
            pltpu.SemaphoreType.REGULAR(((nz // 2).bit_length() - 1,)),
        ],
        compiler_params=pltpu.CompilerParams(
            collective_id=0, has_side_effects=True, vmem_limit_bytes=54 * 1024 * 1024
        ),
        cost_estimate=pl.CostEstimate(flops=1_000_000_000, bytes_accessed=8_000_000, transcendentals=0),
        name="gather_encode_sum",
    )(tokens, key_grad.T, momentum[0], positions, table)
    in_vmem = pl.BlockSpec(memory_space=pltpu.VMEM)
    update, residual, blended = pl.pallas_call(
        second_kernel,
        out_shape=(
            jax.ShapeDtypeStruct((feats, width), jnp.float32),
            jax.ShapeDtypeStruct((feats, width), jnp.float32),
            jax.ShapeDtypeStruct((feats, width), jnp.bfloat16),
        ),
        in_specs=[in_vmem] * 3 + [anywhere] + [in_vmem] * 2,
        out_specs=(anywhere,) * 3,
        scratch_shapes=[
            pltpu.VMEM((feats, width), jnp.float32),
            pltpu.VMEM((feats, width), jnp.bfloat16),
            pltpu.SemaphoreType.DMA((1 + 2 * rows_p,)),
        ],
        compiler_params=pltpu.CompilerParams(vmem_limit_bytes=32 * 1024 * 1024),
        cost_estimate=pl.CostEstimate(flops=300_000_000, bytes_accessed=8_000_000, transcendentals=0),
        name="decode_blend",
    )(total, at, w, residual, key_weight, target)
    return (update, residual[None], blended)


def solution(mesh):
    in_specs = (
        P("rep", "tp"),
        P("rep", "tp"),
        P("rep", "tp", None),
        P("tp", None),
        P("tp", None),
        P("tp", None, None),
    )
    out_specs = (P("tp", None), P("rep", "tp", None), P("tp", None))
    body = functools.partial(shards, NY, mesh.shape["rep"] // NY)
    return jax.shard_map(body, mesh=mesh, in_specs=in_specs, out_specs=out_specs, check_vma=False)
```
